128 devices in a mesh: edge: 128 (over x, y, z, core).
Axes of the slice: x: 4, y: 4, z: 4, core: 2. Of those that a mesh axis runs over, the one named last changes fastest.
Arguments:
- edge_feats: bfloat16 [393216, 512], P('edge'), may hold values from -6 to 6
- node_feats: bfloat16 [40960, 512], P('edge'), may hold values from -6 to 6
- edge_cot: bfloat16 [393216, 512], P('edge'), may hold values from -6 to 6
- node_cot: bfloat16 [40960, 512], P('edge'), may hold values from -6 to 6
- requests: int32 [128, 384], P('edge'), may hold values from 0 to 319, as said below
- send_slot: int32 [3072, 128], P('edge'), may hold values from 0 to 383
- recv_slot: int32 [3072, 128], P('edge'), may hold values from 0 to 383
- w_input: bfloat16 [3, 512, 512], replicated, may hold values from -0.15625 to 0.15625
- w_output: bfloat16 [512, 512], replicated, may hold values from -0.25 to 0.25
- norm_gain: float32 [512], replicated, may hold values from 0.25 to 1.75
Outputs:
- grad_edges: bfloat16 [393216, 512], P('edge')
- grad_nodes: bfloat16 [40960, 512], P('edge')
- grad_w_input: float32 [3, 512, 512], replicated
- grad_w_output: float32 [512, 512], replicated
- grad_gain: float32 [512], replicated
The draws below stay inside these ranges and needn't reach their ends.
Inputs may be any that keep to these rules, and one draw needn't show every extreme that they name: `requests`: within each row, each owner's block of 3 entries holds distinct local node indices.
All inputs are finite; a program needn't handle non-finite values.
Results may differ from the reference program's by a relative error of at most 0.011.
Values may be sent and summed in bfloat16 or wider, within the bound.
No kernel may reach another device: no remote copies, remote signals or barrier semaphores. Data moves between devices by JAX's collectives and lax.ppermute only.
A program may use at most 128 MiB of HBM per device.

```python
import jax
import jax.numpy as jnp
from jax import lax

L = 512
BLK = 128
BLK_DEV = 24
NODE_DEV = 320
CAP = 3
BLOCKS = 3072
EDGES = 393216
NODES = 40960
REQ = 384
N_EDGE = 128


def draw_requests(key, part):
    key = jax.random.fold_in(key, 7)
    pairs = N_EDGE * N_EDGE
    scores = jax.random.randint(key, (pairs, NODE_DEV), 0, 1 << 20) * NODE_DEV
    scores = scores + jnp.arange(NODE_DEV, dtype=jnp.int32)[None, :]
    chosen = jnp.argsort(scores, axis=1)[:, :CAP].astype(jnp.int32)
    return chosen.reshape(N_EDGE, REQ)


def touch_ends(values, own_key, low, high):
    shape = values.shape
    spot = [jax.random.randint(jax.random.fold_in(own_key, axis), (), 0, shape[axis]) for axis in range(len(shape))]
    values = values.at[tuple(spot)].set(low)
    longest = shape.index(max(shape))
    spot[longest] = (spot[longest] + 1) % shape[longest]
    return values.at[tuple(spot)].set(high)


def steps_of(rng, extent, shards, least, high):
    gain, own = 1.0, jax.random.fold_in(rng, 6)
    for axis_at, blocks in shards:
        heights = jnp.exp(jax.random.uniform(jax.random.fold_in(own, axis_at), (blocks,), jnp.float32, least / len(shards), high / len(shards)))
        gain = gain * jnp.repeat(heights, extent[axis_at] // blocks).reshape([-1 if axis == axis_at else 1 for axis in range(len(extent))])
    return gain


def bell_draw(rng, dims, scale, reach, shards=(), kind=jnp.bfloat16):
    gain = steps_of(rng, dims, shards, -0.22, 0.18) if shards else 1.0
    array = jax.random.normal(rng, dims, jnp.float32) * scale * gain
    return jnp.minimum(jnp.maximum(array, -reach), reach).astype(kind)


def setup_inputs(seed: int = 0) -> dict:
    seeds = jax.random.split(jax.random.key(seed), 11)
    edge_feats = bell_draw(seeds[0], (EDGES, L), 1.0, 6.0, ((0, 128),))
    node_feats = bell_draw(seeds[1], (NODES, L), 1.0, 6.0, ((0, 128),))
    edge_cot = bell_draw(seeds[2], (EDGES, L), 1.0, 6.0, ((0, 128),))
    node_cot = bell_draw(seeds[3], (NODES, L), 1.0, 6.0, ((0, 128),))
    requests = draw_requests(jax.random.fold_in(seeds[10], 71), 0)
    send_slot = touch_ends(jax.random.randint(seeds[5], (BLOCKS, BLK), 0, REQ), jax.random.fold_in(seeds[5], 1), 0, REQ - 1).astype(jnp.int32)
    recv_slot = touch_ends(jax.random.randint(seeds[6], (BLOCKS, BLK), 0, REQ), jax.random.fold_in(seeds[6], 1), 0, REQ - 1).astype(jnp.int32)
    w_input = bell_draw(seeds[7], (3, L, L), (3 * L) ** -0.5, 0.15625)
    w_output = bell_draw(seeds[8], (L, L), L ** -0.5, 0.25)
    norm_gain = jnp.clip(1.0 + 0.15 * jax.random.normal(seeds[9], (L,), jnp.float32), 0.25, 1.75)
    return {"edge_feats": edge_feats, "node_feats": node_feats, "edge_cot": edge_cot, "node_cot": node_cot, "requests": requests, "send_slot": send_slot, "recv_slot": recv_slot, "w_input": w_input, "w_output": w_output, "norm_gain": norm_gain}


def contract_rows(left, right):
    return lax.dot_general(left, right, (((0,), (0,)), ((), ())), preferred_element_type=jnp.float32)

def contract_cols(left, right):
    return lax.dot_general(left, right, (((1,), (1,)), ((), ())), preferred_element_type=jnp.float32)

def edge_forward(edge_rows, send_rows, recv_rows, w_input, w_output):
    preact = jnp.dot(edge_rows, w_input[0], preferred_element_type=jnp.float32)
    preact = preact + jnp.dot(send_rows, w_input[1], preferred_element_type=jnp.float32)
    preact = preact + jnp.dot(recv_rows, w_input[2], preferred_element_type=jnp.float32)
    hidden = jax.nn.silu(preact).astype(jnp.bfloat16)
    mixed_out = jnp.dot(hidden, w_output, preferred_element_type=jnp.float32)
    center = mixed_out - lax.optimization_barrier(jnp.mean(mixed_out, axis=-1, keepdims=True))
    variance = lax.optimization_barrier(jnp.mean(center * center, axis=-1, keepdims=True))
    inverse = lax.rsqrt(variance + 1e-05)
    return (preact, hidden, center * inverse, inverse)

def edge_grads(saved, edge_rows, send_rows, recv_rows, edge_grad, recv_grad, w_input, w_output, norm_gain):
    preact, hidden, normed, inverse = saved
    upstream = edge_grad.astype(jnp.float32) + recv_grad.astype(jnp.float32)
    scaled = upstream * norm_gain
    d_mixed = inverse * (scaled - lax.optimization_barrier(jnp.mean(scaled, axis=-1, keepdims=True)) - normed * lax.optimization_barrier(jnp.mean(scaled * normed, axis=-1, keepdims=True)))
    d_mixed = d_mixed.astype(jnp.bfloat16)
    part_gain = lax.optimization_barrier(jnp.sum(upstream * normed, axis=0))
    part_output = contract_rows(hidden, d_mixed)
    d_hidden = contract_cols(d_mixed, w_output)
    logistic = jax.nn.sigmoid(preact)
    d_preact = (d_hidden * logistic * (1.0 + preact * (1.0 - logistic))).astype(jnp.bfloat16)
    part_input = jnp.stack([contract_rows(operand, d_preact) for operand in (edge_rows, send_rows, recv_rows)])
    grad_edge = (edge_grad.astype(jnp.float32) + contract_cols(d_preact, w_input[0])).astype(jnp.bfloat16)
    send_part = contract_cols(d_preact, w_input[1])
    recv_part = contract_cols(d_preact, w_input[2])
    return (grad_edge, send_part, recv_part, part_input, part_output, part_gain)

def reference(edge_feats, node_feats, edge_cot, node_cot, requests, send_slot, recv_slot, w_input, w_output, norm_gain):
    owners = jnp.arange(REQ, dtype=jnp.int32) // CAP
    edge_split = edge_feats.reshape(N_EDGE, BLK_DEV * BLK, L)
    cot_split = edge_cot.reshape(N_EDGE, BLK_DEV * BLK, L)
    send_split = send_slot.reshape(N_EDGE, BLK_DEV * BLK)
    recv_split = recv_slot.reshape(N_EDGE, BLK_DEV * BLK)

    def per_device(running, pieces):
        node_sums, sum_input, sum_output, sum_gain = running
        edge_rows, edge_grad, send_here, recv_here, wanted = pieces
        slot_nodes = (owners * NODE_DEV + wanted).astype(jnp.int32)
        sender = slot_nodes[send_here]
        receiver = slot_nodes[recv_here]
        send_rows = node_feats[sender]
        recv_rows = node_feats[receiver]
        saved = edge_forward(edge_rows, send_rows, recv_rows, w_input, w_output)
        grad_edge, send_part, recv_part, part_input, part_output, part_gain = edge_grads(saved, edge_rows, send_rows, recv_rows, edge_grad, node_cot[receiver], w_input, w_output, norm_gain)
        node_sums = node_sums.at[sender].add(send_part).at[receiver].add(recv_part)
        return ((node_sums, sum_input + part_input, sum_output + part_output, sum_gain + part_gain), grad_edge)
    start = (jnp.zeros((NODES, L), jnp.float32), jnp.zeros((3, L, L), jnp.float32), jnp.zeros((L, L), jnp.float32), jnp.zeros((L,), jnp.float32))
    final, grad_split = lax.scan(per_device, start, (edge_split, cot_split, send_split, recv_split, requests))
    node_sums, sum_input, sum_output, sum_gain = final
    grad_nodes = (node_cot.astype(jnp.float32) + node_sums).astype(jnp.bfloat16)
    factor = float(EDGES) ** (-0.5)
    return (grad_split.reshape(EDGES, L), grad_nodes, sum_input * factor, sum_output * factor, sum_gain * factor)
```

```python
import functools

import jax
import jax.numpy as jnp
from jax import lax
from jax.experimental import pallas as pl
from jax.experimental.pallas import tpu as pltpu
from jax.sharding import Mesh, PartitionSpec as P

BF = jnp.bfloat16
F32 = jnp.float32
LANES = 128
CORES = 2
VMEM_BYTES = 56 * 1024 * 1024


def dot(left, right, over=((1,), (0,))):
    return lax.dot_general(left, right, (over, ((), ())), preferred_element_type=F32)


def whole(shape):
    return pl.BlockSpec(shape, lambda *_: (0,) * len(shape))


def smem():
    return pl.BlockSpec(memory_space=pltpu.SMEM)


def one_hot(left, right):
    return jnp.where(left == right, 1.0, 0.0).astype(BF)


def pick_kernel(asked_ref, feats_ref, cots_ref, out_ref, rows):
    devices, cap = asked_ref.shape
    nodes, width = feats_ref.shape
    blocks = width // LANES
    per = cap * 2 * blocks
    spot = lax.broadcasted_iota(jnp.int32, (devices, nodes), 1)
    for k in range(cap):
        hot = one_hot(asked_ref[:, k : k + 1], spot)
        for at, table in enumerate((feats_ref, cots_ref)):
            found = dot(hot, table[...])
            for j in range(blocks):
                rows[pl.ds(k * 2 * blocks + at * blocks + j, devices, stride=per), :] = found[
                    :, j * LANES : (j + 1) * LANES
                ]
    out_ref[...] = rows[...].astype(BF)


def pick_rows(asked, feats, cots):
    devices, cap = asked.shape
    width = feats.shape[1]
    total = devices * cap * 2 * width // LANES
    return pl.pallas_call(
        pick_kernel,
        out_shape=jax.ShapeDtypeStruct((total, LANES), BF),
        scratch_shapes=[pltpu.VMEM((total, LANES), F32)],
        compiler_params=pltpu.CompilerParams(vmem_limit_bytes=VMEM_BYTES),
        name="pick_rows",
    )(asked, feats, cots)


def slot_ids(position, chips, cap):
    half = cap * chips
    core = jnp.where(position >= half, 1, 0)
    rest = position - core * half
    k = jnp.where(rest >= chips, 1, 0) + jnp.where(rest >= 2 * chips, 1, 0)
    chip = rest - k * chips
    return chip * (CORES * cap) + core * cap + k


def edge_kernel(
    cap,
    core_ref,
    send_ref,
    recv_ref,
    rows_ref,
    w_in_ref,
    w_out_ref,
    gain_ref,
    feats_ref,
    cot_ref,
    grad_ref,
    own_ref,
    other_ref,
    rows32,
    feat_tab,
    cot_tab,
    pre_tab,
    sums,
    grads,
    gain_sum,
    nodes,
    tail,
):
    step, steps = pl.program_id(0), pl.num_programs(0)
    tile, width = feats_ref.shape
    slots = feat_tab.shape[0]
    chips = slots // (cap * CORES)
    blocks = width // LANES
    per = cap * 2 * blocks

    @pl.when(step == 0)
    def _():
        rows32[...] = rows_ref[...].astype(F32)
        for core in range(CORES):
            for k in range(cap):
                at = (core * cap + k) * chips
                for j in range(blocks):
                    cols = slice(j * LANES, (j + 1) * LANES)
                    first = core * per + k * 2 * blocks + j
                    feat_tab[at : at + chips, cols] = rows32[
                        pl.ds(first, chips, stride=CORES * per), :
                    ].astype(BF)
                    cot_tab[at : at + chips, cols] = rows32[
                        pl.ds(first + blocks, chips, stride=CORES * per), :
                    ].astype(BF)
        for part in range(2):
            pre_tab[part * slots : (part + 1) * slots, :] = dot(
                feat_tab[...], w_in_ref[part + 1]
            ).astype(BF)
        sums[...] = jnp.zeros_like(sums)
        grads[...] = jnp.zeros_like(grads)
        gain_sum[...] = jnp.zeros_like(gain_sum)

    lane_ids = slot_ids(lax.broadcasted_iota(jnp.int32, (1, slots), 1), chips, cap)
    row_ids = slot_ids(lax.broadcasted_iota(jnp.int32, (slots, LANES), 0), chips, cap)
    groups = tile // LANES
    hot_rows, hot_cols = [], []
    for ref in (send_ref, recv_ref):
        found_rows, found_cols = [], []
        for g in range(groups):
            line = ref[pl.ds(step * groups + g, 1), :]
            found_cols.append(one_hot(row_ids, line))
            upright = jnp.broadcast_to(line, (LANES, LANES)).T
            found_rows.append(
                jnp.concatenate(
                    [
                        one_hot(upright, lane_ids[:, b * LANES : (b + 1) * LANES])
                        for b in range(slots // LANES)
                    ],
                    axis=1,
                )
            )
        hot_rows.append(jnp.concatenate(found_rows, axis=0))
        hot_cols.append(jnp.concatenate(found_cols, axis=1))
    both_rows = jnp.concatenate(hot_rows, axis=1)
    both_cols = jnp.concatenate(hot_cols, axis=0)

    feats = feats_ref[...]
    preact = dot(feats, w_in_ref[0]) + dot(both_rows, pre_tab[...])
    logistic = 0.5 * jnp.tanh(0.5 * preact) + 0.5
    silu = preact * logistic
    hidden = silu.astype(BF)
    slope = logistic + silu * (1.0 - logistic)
    mixed = dot(hidden, w_out_ref[...])
    center = mixed - jnp.mean(mixed, axis=1, keepdims=True)
    inverse = lax.rsqrt(jnp.mean(center * center, axis=1, keepdims=True) + 1e-5)
    normed = center * inverse
    cots = cot_ref[...].astype(F32)
    upstream = cots + dot(hot_rows[1], cot_tab[...])
    scaled = upstream * gain_ref[...]
    d_mixed = (
        inverse
        * (
            scaled
            - jnp.mean(scaled, axis=1, keepdims=True)
            - normed * jnp.mean(scaled * normed, axis=1, keepdims=True)
        )
    ).astype(BF)
    product = upstream * normed
    gain_sum[...] += jnp.sum(product.reshape(tile // 8, 8, width), axis=0)
    d_hidden = dot(d_mixed, w_out_ref[...], ((1,), (1,)))
    d_preact = (d_hidden * slope).astype(BF)
    grad_ref[...] = (cots + dot(d_preact, w_in_ref[0], ((1,), (1,)))).astype(BF)
    sums[...] += dot(both_cols, d_preact)
    grads[0:width, :] += dot(feats, d_preact, ((0,), (0,)))
    grads[3 * width : 4 * width, :] += dot(hidden, d_mixed, ((0,), (0,)))

    @pl.when(step == steps - 1)
    def _():
        sender = sums[0:slots, :].astype(BF)
        receiver = sums[slots : 2 * slots, :].astype(BF)
        nodes[...] = dot(sender, w_in_ref[1], ((1,), (1,))) + dot(
            receiver, w_in_ref[2], ((1,), (1,))
        )
        grads[width : 2 * width, :] = dot(feat_tab[...], sender, ((0,), (0,)))
        grads[2 * width : 3 * width, :] = dot(feat_tab[...], receiver, ((0,), (0,)))
        gain = jnp.sum(gain_sum[...], axis=0, keepdims=True)
        core = core_ref[0]
        piece = 2 * width // chips
        body = piece * blocks
        for target, which in ((own_ref, core), (other_ref, 1 - core)):
            first = pl.multiple_of(which * (2 * width), 2 * width)
            for j in range(blocks):
                cols = slice(j * LANES, (j + 1) * LANES)
                target[:, j * piece : (j + 1) * piece, :] = (
                    grads[pl.ds(first, 2 * width), cols].reshape(chips, piece, LANES).astype(BF)
                )
                for k in range(cap):
                    begin = pl.multiple_of(which * (cap * chips) + k * chips, chips)
                    tail[pl.ds(k * blocks + j, chips, stride=16), :] = nodes[
                        pl.ds(begin, chips), cols
                    ]
                tail[pl.ds(cap * blocks + j, chips, stride=16), :] = jnp.broadcast_to(
                    gain[:, cols], (chips, LANES)
                )
            target[:, body : body + 16, :] = tail[...].reshape(chips, 16, LANES).astype(BF)


def edge_pass(core, send_slot, recv_slot, rows, w_input, w_output, gain, feats, cot, cap, tile):
    edges, width = feats.shape
    devices = rows.shape[0] * LANES // (cap * 2 * width)
    chips = devices // CORES
    slots = devices * cap
    blocks = width // LANES
    packet = 2 * width // chips * blocks + 16
    tiles = pl.BlockSpec((tile, width), lambda i: (i, 0))
    packets = jax.ShapeDtypeStruct((chips, packet, LANES), BF)
    return pl.pallas_call(
        functools.partial(edge_kernel, cap),
        grid=(edges // tile,),
        in_specs=[
            smem(),
            whole(send_slot.shape),
            whole(recv_slot.shape),
            whole(rows.shape),
            whole(w_input.shape),
            whole(w_output.shape),
            whole(gain.shape),
            tiles,
            tiles,
        ],
        out_specs=[tiles, whole(packets.shape), whole(packets.shape)],
        out_shape=[jax.ShapeDtypeStruct(feats.shape, BF), packets, packets],
        scratch_shapes=[
            pltpu.VMEM(rows.shape, F32),
            pltpu.VMEM((slots, width), BF),
            pltpu.VMEM((slots, width), BF),
            pltpu.VMEM((2 * slots, width), BF),
            pltpu.VMEM((2 * slots, width), F32),
            pltpu.VMEM((4 * width, width), F32),
            pltpu.VMEM((8, width), F32),
            pltpu.VMEM((slots, width), F32),
            pltpu.VMEM((chips * 16, LANES), F32),
        ],
        compiler_params=pltpu.CompilerParams(vmem_limit_bytes=VMEM_BYTES),
        name="edge_pass",
    )(core, send_slot, recv_slot, rows, w_input, w_output, gain, feats, cot)


def merge_kernel(own_ref, got_ref, out_ref):
    body = own_ref.shape[1] - 16
    out_ref[:, 0:body, :] = (
        own_ref[:, 0:body, :].astype(F32) + got_ref[:, 0:body, :].astype(F32)
    ).astype(BF)
    out_ref[:, body : body + 16, :] = own_ref[:, body : body + 16, :]
    out_ref[:, body + 16 : body + 32, :] = got_ref[:, body : body + 16, :]


def merge(own, got):
    chips, packet, _ = own.shape
    step = 8
    spec = pl.BlockSpec((step, packet, LANES), lambda i: (i, 0, 0))
    return pl.pallas_call(
        merge_kernel,
        grid=(chips // step,),
        in_specs=[spec, spec],
        out_specs=pl.BlockSpec((step, packet + 16, LANES), lambda i: (i, 0, 0)),
        out_shape=jax.ShapeDtypeStruct((chips, packet + 16, LANES), BF),
        name="merge",
    )(own, got)


def reduce_kernel(factor, gain_row, in_ref, out_ref, gain_ref):
    chips, packet, _ = in_ref.shape
    body = packet - 32
    total = jnp.sum(in_ref[:, 0:body, :].astype(F32), axis=0) * factor
    out_ref[...] = jnp.broadcast_to(total.astype(BF)[None], out_ref.shape)
    ends = jnp.sum(
        in_ref[:, body : body + 16, :].astype(F32) + in_ref[:, body + 16 : body + 32, :].astype(F32),
        axis=0,
    )
    gain_ref[...] = ends[gain_row:16, :] * factor


def reduce_packets(packets, factor, gain_row):
    chips, packet, _ = packets.shape
    return pl.pallas_call(
        functools.partial(reduce_kernel, factor, gain_row),
        out_shape=[
            jax.ShapeDtypeStruct((chips, packet - 32, LANES), BF),
            jax.ShapeDtypeStruct((16 - gain_row, LANES), F32),
        ],
        compiler_params=pltpu.CompilerParams(vmem_limit_bytes=VMEM_BYTES),
        name="reduce_packets",
    )(packets)


def node_kernel(core_ref, asked_ref, packets_ref, cots_ref, out_ref, ends, rows, hots):
    devices, cap = asked_ref.shape
    nodes, width = cots_ref.shape
    chips = devices // CORES
    blocks = width // LANES
    body = packets_ref.shape[1] - 32
    ends[...] = packets_ref[:, body : body + 32, :].astype(F32).reshape(chips * 32, LANES)
    spot = lax.broadcasted_iota(jnp.int32, (chips, nodes), 1)
    core = core_ref[0]
    for flag in range(CORES):
        asker = core if flag == 0 else 1 - core
        asked = asked_ref[pl.ds(asker, chips, stride=CORES), :]
        for k in range(cap):
            at = (flag * cap + k) * chips
            hots[at : at + chips, :] = one_hot(asked[:, k : k + 1], spot)
            for j in range(blocks):
                rows[at : at + chips, j * LANES : (j + 1) * LANES] = ends[
                    pl.ds(flag * 16 + k * blocks + j, chips, stride=32), :
                ].astype(BF)
    sums = dot(hots[...], rows[...], ((0,), (0,)))
    out_ref[...] = (cots_ref[...].astype(F32) + sums).astype(BF)


def node_grads(core, asked, packets, cots):
    devices, cap = asked.shape
    nodes, width = cots.shape
    slots = devices * cap
    vmem = pl.BlockSpec(memory_space=pltpu.VMEM)
    return pl.pallas_call(
        node_kernel,
        in_specs=[smem(), vmem, vmem, vmem],
        out_specs=vmem,
        out_shape=jax.ShapeDtypeStruct(cots.shape, BF),
        scratch_shapes=[
            pltpu.VMEM((devices // CORES * 32, LANES), F32),
            pltpu.VMEM((slots, width), BF),
            pltpu.VMEM((slots, nodes), BF),
        ],
        compiler_params=pltpu.CompilerParams(vmem_limit_bytes=VMEM_BYTES),
        name="node_grads",
    )(core, asked, packets, cots)


def unpack_kernel(core_ref, mine_ref, other_ref, input_ref, output_ref):
    chips, body, _ = mine_ref.shape
    width = output_ref.shape[0]
    blocks = width // LANES
    piece = body // blocks

    def write(low, high):
        for j in range(blocks):
            cols = slice(j * LANES, (j + 1) * LANES)
            lower = low[:, j * piece : (j + 1) * piece, :].astype(F32).reshape(2 * width, LANES)
            upper = high[:, j * piece : (j + 1) * piece, :].astype(F32).reshape(2 * width, LANES)
            input_ref[0 : 2 * width, cols] = lower
            input_ref[2 * width : 3 * width, cols] = upper[0:width]
            output_ref[:, cols] = upper[width : 2 * width]

    @pl.when(core_ref[0] == 0)
    def _():
        write(mine_ref, other_ref)

    @pl.when(core_ref[0] != 0)
    def _():
        write(other_ref, mine_ref)


def unpack(core, mine, other, width):
    vmem = pl.BlockSpec(memory_space=pltpu.VMEM)
    return pl.pallas_call(
        unpack_kernel,
        in_specs=[smem(), vmem, vmem],
        out_specs=[vmem, vmem],
        out_shape=[
            jax.ShapeDtypeStruct((3 * width, width), F32),
            jax.ShapeDtypeStruct((width, width), F32),
        ],
        compiler_params=pltpu.CompilerParams(vmem_limit_bytes=VMEM_BYTES),
        name="unpack",
    )(core, mine, other)


def on_device(
    edge_feats,
    node_feats,
    edge_cot,
    node_cot,
    requests,
    send_slot,
    recv_slot,
    w_input,
    w_output,
    norm_gain,
):
    chips, cores = lax.axis_size("chip"), lax.axis_size("core")
    devices = chips * cores
    both = ("chip", "core")
    cap = requests.shape[1] // devices
    edges, width = edge_feats.shape
    core = lax.axis_index("core").astype(jnp.int32).reshape(1)
    pairs = [(d, d ^ 1) for d in range(devices)]

    asked = lax.all_to_all(
        requests.reshape(devices, 1, cap), both, split_axis=0, concat_axis=0, tiled=True
    ).reshape(devices, cap)
    picked = pick_rows(asked, node_feats, node_cot).reshape(devices, -1, LANES)
    rows = lax.all_to_all(picked, both, split_axis=0, concat_axis=0, tiled=True).reshape(-1, LANES)
    grad_edges, own, other = edge_pass(
        core,
        send_slot,
        recv_slot,
        rows,
        w_input,
        w_output,
        norm_gain.reshape(1, width),
        edge_feats,
        edge_cot,
        cap,
        512,
    )
    got = lax.ppermute(other, both, pairs)
    packets = lax.all_to_all(merge(own, got), "chip", split_axis=0, concat_axis=0, tiled=True)
    factor = float(edges * devices) ** (-0.5)
    pieces, gain = reduce_packets(packets, factor, cap * width // LANES)
    mine = lax.all_to_all(pieces, "chip", split_axis=0, concat_axis=0, tiled=True)
    grad_nodes = node_grads(core, asked, packets, node_cot)
    partner = lax.ppermute(mine, both, pairs)
    grad_input, grad_output = unpack(core, mine, partner, width)
    return (
        grad_edges,
        grad_nodes,
        grad_input.reshape(3, width, width),
        grad_output,
        gain.reshape(width),
    )


def solution(mesh):
    pairs = Mesh(mesh.devices.reshape(-1, CORES), ("chip", "core"))
    rows = P(("chip", "core"), None)
    return jax.shard_map(
        on_device,
        mesh=pairs,
        in_specs=(rows,) * 7 + (P(),) * 3,
        out_specs=(rows, rows, P(), P(), P()),
        check_vma=False,
    )
```

```python
import functools

import jax
import jax.numpy as jnp
from jax import lax
from jax.experimental import pallas as pl
from jax.experimental.pallas import tpu as pltpu
from jax.sharding import Mesh, PartitionSpec as P

BF = jnp.bfloat16
F32 = jnp.float32
LANES = 128
CORES = 2
TILE = 768
PRE = F32
BIG_VMEM = 48 * 1024 * 1024
VMEM = pl.BlockSpec(memory_space=pltpu.VMEM)


def dot(left, right, over=((1,), (0,))):
    return lax.dot_general(left, right, (over, ((), ())), preferred_element_type=F32)


def whole(shape):
    return pl.BlockSpec(shape, lambda *_: (0,) * len(shape))


def smem():
    return pl.BlockSpec(memory_space=pltpu.SMEM)


def cost(flops, moved):
    return pl.CostEstimate(flops=flops, bytes_accessed=moved, transcendentals=0)


def one_hot(left, right):
    return jnp.where(left == right, 1.0, 0.0).astype(BF)


def pick_kernel(asked_ref, feats_ref, cots_ref, out_ref, rows):
    devices, cap = asked_ref.shape
    nodes, width = feats_ref.shape
    blocks = width // LANES
    per = cap * 2 * blocks
    spot = lax.broadcasted_iota(jnp.int32, (devices, nodes), 1)
    for k in range(cap):
        hot = one_hot(asked_ref[:, k : k + 1], spot)
        for at, table in enumerate((feats_ref, cots_ref)):
            found = dot(hot, table[...])
            for j in range(blocks):
                rows[pl.ds(k * 2 * blocks + at * blocks + j, devices, stride=per), :] = found[
                    :, j * LANES : (j + 1) * LANES
                ]
    out_ref[...] = rows[...].astype(BF)


def pick_rows(asked, feats, cots):
    devices, cap = asked.shape
    width = feats.shape[1]
    total = devices * cap * 2 * width // LANES
    return pl.pallas_call(
        pick_kernel,
        out_shape=jax.ShapeDtypeStruct((total, LANES), BF),
        scratch_shapes=[pltpu.VMEM((total, LANES), F32)],
        compiler_params=pltpu.CompilerParams(vmem_limit_bytes=BIG_VMEM),
        cost_estimate=cost(4 * devices * cap * feats.size, 4 * total * LANES),
        name="pick_rows",
    )(asked, feats, cots)


def slot_ids(position, chips, cap):
    half = cap * chips
    core = jnp.where(position >= half, 1, 0)
    rest = position - core * half
    k = jnp.where(rest >= chips, 1, 0) + jnp.where(rest >= 2 * chips, 1, 0)
    chip = rest - k * chips
    return chip * (CORES * cap) + core * cap + k


def prep_kernel(feats_ref, w_ref, pre_ref, turned_ref):
    feats = feats_ref[...]
    pre_ref[...] = dot(feats, w_ref[0]).astype(PRE)
    turned_ref[0] = feats.T


def prep_pass(feats, w_input, tile):
    edges, width = feats.shape
    tiles = edges // tile
    rows = pl.BlockSpec((tile, width), lambda i: (i, 0))
    return pl.pallas_call(
        prep_kernel,
        grid=(tiles,),
        in_specs=[rows, pl.BlockSpec((1, width, width), lambda i: (0, 0, 0))],
        out_specs=[rows, pl.BlockSpec((1, width, tile), lambda i: (i, 0, 0))],
        out_shape=[
            jax.ShapeDtypeStruct((edges, width), PRE),
            jax.ShapeDtypeStruct((tiles, width, tile), BF),
        ],
        compiler_params=pltpu.CompilerParams(vmem_limit_bytes=BIG_VMEM),
        cost_estimate=cost(2 * edges * width * width, 8 * feats.size),
        name="prep_pass",
    )(feats, w_input)


def grad_kernel(d_preact_ref, w_ref, cot_ref, out_ref):
    grad = dot(d_preact_ref[...], w_ref[0], ((1,), (1,)))
    out_ref[...] = (cot_ref[...].astype(F32) + grad).astype(BF)


def grad_pass(d_preact, w_input, cot, tile):
    edges, width = cot.shape
    tiles = pl.BlockSpec((tile, width), lambda i: (i, 0))
    return pl.pallas_call(
        grad_kernel,
        grid=(edges // tile,),
        in_specs=[tiles, pl.BlockSpec((1, width, width), lambda i: (0, 0, 0)), tiles],
        out_specs=tiles,
        out_shape=jax.ShapeDtypeStruct(cot.shape, BF),
        cost_estimate=cost(2 * edges * width * width, 6 * cot.size),
        name="grad_pass",
    )(d_preact, w_input, cot)


def edge_kernel(
    cap,
    core_ref,
    send_ref,
    recv_ref,
    gain_ref,
    rows_hbm,
    w_in_hbm,
    w_out_hbm,
    pre_hbm,
    turned_hbm,
    cot_hbm,
    d_preact_hbm,
    own_ref,
    other_ref,
    sums_ref,
    rows16,
    rows32,
    w_in,
    w_out,
    pre,
    turned,
    cot,
    d_preact,
    feat_tab,
    cot_tab,
    pre_tab,
    hot_rows,
    hot_cols,
    hidden,
    d_mixed,
    sums,
    grads,
    gain_sum,
    once,
    per_tile,
):
    tiles, _, tile = turned.shape
    slots, width = feat_tab.shape
    chips = slots // (cap * CORES)
    blocks = width // LANES
    per = cap * 2 * blocks
    groups = tile // LANES

    def span(t):
        return pl.ds(pl.multiple_of(t * tile, tile), tile)

    first = (
        pltpu.make_async_copy(rows_hbm, rows16, once.at[0]),
        pltpu.make_async_copy(w_in_hbm.at[pl.ds(1, 2)], w_in, once.at[1]),
        pltpu.make_async_copy(w_out_hbm, w_out, once.at[2]),
    )

    def load(t):
        return (
            pltpu.make_async_copy(pre_hbm.at[span(t)], pre.at[span(t)], per_tile.at[0, t]),
            pltpu.make_async_copy(cot_hbm.at[span(t)], cot.at[span(t)], per_tile.at[1, t]),
            pltpu.make_async_copy(turned_hbm.at[t], turned.at[t], per_tile.at[2, t]),
        )

    def leave(t):
        return pltpu.make_async_copy(d_preact.at[span(t)], d_preact_hbm.at[span(t)], per_tile.at[3, t])

    for copy in first:
        copy.start()
    for copy in load(0):
        copy.start()

    lane_ids = slot_ids(lax.broadcasted_iota(jnp.int32, (1, slots), 1), chips, cap)
    row_ids = slot_ids(lax.broadcasted_iota(jnp.int32, (slots, LANES), 0), chips, cap)

    def mark_rows(t):
        for g in range(groups):
            for at, ref in enumerate((send_ref, recv_ref)):
                upright = jnp.broadcast_to(ref[pl.ds(t * groups + g, 1), :], (LANES, LANES)).T
                for b in range(slots // LANES):
                    hot_rows[g * LANES : (g + 1) * LANES, at * slots + b * LANES : at * slots + (b + 1) * LANES] = (
                        one_hot(upright, lane_ids[:, b * LANES : (b + 1) * LANES])
                    )

    def mark_cols(t):
        for g in range(groups):
            for at, ref in enumerate((send_ref, recv_ref)):
                hot_cols[at * slots : (at + 1) * slots, g * LANES : (g + 1) * LANES] = one_hot(
                    row_ids, ref[pl.ds(t * groups + g, 1), :]
                )

    sums[...] = jnp.zeros_like(sums)
    grads[0:width, :] = jnp.zeros((width, width), F32)
    grads[3 * width : 4 * width, :] = jnp.zeros((width, width), F32)
    gain_sum[...] = jnp.zeros_like(gain_sum)
    mark_rows(0)
    first[0].wait()
    rows32[...] = rows16[...].astype(F32)
    for core in range(CORES):
        for k in range(cap):
            at = (core * cap + k) * chips
            for j in range(blocks):
                cols = slice(j * LANES, (j + 1) * LANES)
                begin = core * per + k * 2 * blocks + j
                feat_tab[at : at + chips, cols] = rows32[pl.ds(begin, chips, stride=CORES * per), :].astype(BF)
                cot_tab[at : at + chips, cols] = rows32[
                    pl.ds(begin + blocks, chips, stride=CORES * per), :
                ].astype(BF)
    first[1].wait()
    for t in range(1, tiles):
        for copy in load(t):
            copy.start()
    for part in range(2):
        pre_tab[part * slots : (part + 1) * slots, :] = dot(feat_tab[...], w_in[part]).astype(BF)
    first[2].wait()
    for copy in load(0):
        copy.wait()

    def contract(t):
        mark_cols(t)
        arrived = d_preact[span(t), :]
        sums[...] += dot(hot_cols[...], arrived)
        grads[0:width, :] += dot(turned[t], arrived)
        grads[3 * width : 4 * width, :] += dot(hidden[...], d_mixed[...], ((0,), (0,)))

    def chain(t):
        preact = pre[span(t), :].astype(F32) + dot(hot_rows[...], pre_tab[...])
        logistic = 0.5 * jnp.tanh(0.5 * preact) + 0.5
        silu = preact * logistic
        rounded = silu.astype(BF)
        hidden[...] = rounded
        slope = logistic + silu * (1.0 - logistic)
        mixed = dot(rounded, w_out[...])
        center = mixed - jnp.mean(mixed, axis=1, keepdims=True)
        inverse = lax.rsqrt(jnp.mean(center * center, axis=1, keepdims=True) + 1e-5)
        normed = center * inverse
        upstream = cot[span(t), :].astype(F32) + dot(hot_rows[:, slots:], cot_tab[...])
        scaled = upstream * gain_ref[...]
        turned_back = (
            inverse
            * (
                scaled
                - jnp.mean(scaled, axis=1, keepdims=True)
                - normed * jnp.mean(scaled * normed, axis=1, keepdims=True)
            )
        ).astype(BF)
        gain_sum[...] += jnp.sum((upstream * normed).reshape(tile // 8, 8, width), axis=0)
        d_mixed[...] = turned_back
        d_hidden = dot(turned_back, w_out[...], ((1,), (1,)))
        d_preact[span(t), :] = (d_hidden * slope).astype(BF)

    chain(0)

    @pl.loop(1, tiles)
    def _(t):
        for copy in load(t):
            copy.wait()
        leave(t - 1).start()
        contract(t - 1)
        mark_rows(t)
        chain(t)

    leave(tiles - 1).start()
    contract(tiles - 1)

    sums_ref[...] = sums[...].astype(BF)
    for part in range(2):
        grads[(part + 1) * width : (part + 2) * width, :] = dot(
            feat_tab[...], sums_ref[part * slots : (part + 1) * slots, :], ((0,), (0,))
        )
    gain = jnp.sum(gain_sum[...], axis=0, keepdims=True)
    core = core_ref[0]
    piece = 2 * width // chips
    body = piece * blocks
    for target, which in ((other_ref, 1 - core), (own_ref, core)):
        begin = pl.multiple_of(which * (2 * width), 2 * width)
        for j in range(blocks):
            target[:, j * piece : (j + 1) * piece, :] = (
                grads[pl.ds(begin, 2 * width), j * LANES : (j + 1) * LANES]
                .reshape(chips, piece, LANES)
                .astype(BF)
            )
        lines = [jnp.broadcast_to(gain[:, j * LANES : (j + 1) * LANES], (2, LANES)) for j in range(blocks)]
        target[:, body:, :] = jnp.broadcast_to(jnp.concatenate(lines, axis=0)[None].astype(BF), (chips, 8, LANES))
    for t in range(tiles):
        leave(t).wait()


def edge_pass(core, send_slot, recv_slot, gain, rows, w_input, w_output, pre, turned, cot, cap):
    edges, width = cot.shape
    tiles, _, tile = turned.shape
    devices = rows.shape[0] * LANES // (cap * 2 * width)
    slots = devices * cap
    chips = devices // CORES
    packets = jax.ShapeDtypeStruct((chips, 2 * width // chips * (width // LANES) + 8, LANES), BF)
    anywhere = pl.BlockSpec(memory_space=pl.ANY)
    return pl.pallas_call(
        functools.partial(edge_kernel, cap),
        in_specs=[smem()] + [VMEM] * 3 + [anywhere] * 6,
        out_specs=[anywhere] + [VMEM] * 3,
        out_shape=[
            jax.ShapeDtypeStruct(cot.shape, BF),
            packets,
            packets,
            jax.ShapeDtypeStruct((2 * slots, width), BF),
        ],
        scratch_shapes=[
            pltpu.VMEM(rows.shape, BF),
            pltpu.VMEM(rows.shape, F32),
            pltpu.VMEM((2, width, width), BF),
            pltpu.VMEM((width, width), BF),
            pltpu.VMEM(pre.shape, pre.dtype),
            pltpu.VMEM(turned.shape, BF),
            pltpu.VMEM(cot.shape, BF),
            pltpu.VMEM(cot.shape, BF),
            pltpu.VMEM((slots, width), BF),
            pltpu.VMEM((slots, width), BF),
            pltpu.VMEM((2 * slots, width), BF),
            pltpu.VMEM((tile, 2 * slots), BF),
            pltpu.VMEM((2 * slots, tile), BF),
            pltpu.VMEM((tile, width), BF),
            pltpu.VMEM((tile, width), BF),
            pltpu.VMEM((2 * slots, width), F32),
            pltpu.VMEM((4 * width, width), F32),
            pltpu.VMEM((8, width), F32),
            pltpu.SemaphoreType.DMA((3,)),
            pltpu.SemaphoreType.DMA((4, tiles)),
        ],
        compiler_params=pltpu.CompilerParams(vmem_limit_bytes=BIG_VMEM),
        cost_estimate=cost(16 * edges * width * width, 8 * cot.size),
        name="edge_pass",
    )(core, send_slot, recv_slot, gain, rows, w_input, w_output, pre, turned, cot)


def back_kernel(cap, core_ref, sums_ref, w_ref, own_ref, other_ref, tail):
    slots = sums_ref.shape[0] // 2
    width = sums_ref.shape[1]
    chips = slots // (cap * CORES)
    blocks = width // LANES
    nodes = dot(sums_ref[0:slots, :], w_ref[1], ((1,), (1,))) + dot(
        sums_ref[slots : 2 * slots, :], w_ref[2], ((1,), (1,))
    )
    core = core_ref[0]
    tail[...] = jnp.zeros_like(tail)
    for side in range(CORES):
        for k in range(cap):
            at = (side * cap + k) * chips
            for j in range(blocks):
                tail[side, pl.ds(core * (cap * blocks) + k * blocks + j, chips, stride=CORES * cap * blocks), :] = (
                    nodes[at : at + chips, j * LANES : (j + 1) * LANES]
                )
    own_ref[...] = tail[core].astype(BF).reshape(own_ref.shape)
    other_ref[...] = tail[1 - core].astype(BF).reshape(other_ref.shape)


def back_rows(core, sums, w_input, cap):
    slots, width = sums.shape[0] // 2, sums.shape[1]
    chips = slots // (cap * CORES)
    lines = CORES * cap * width // LANES
    return pl.pallas_call(
        functools.partial(back_kernel, cap),
        in_specs=[smem(), VMEM, VMEM],
        out_specs=[VMEM] * 2,
        out_shape=[jax.ShapeDtypeStruct((chips, lines, LANES), BF)] * 2,
        scratch_shapes=[pltpu.VMEM((CORES, chips * lines, LANES), F32)],
        compiler_params=pltpu.CompilerParams(vmem_limit_bytes=BIG_VMEM),
        cost_estimate=cost(2 * sums.size * width, 6 * sums.size),
        name="back_rows",
    )(core, sums, w_input)


def reduce_kernel(factor, in_ref, own_ref, got_ref, out_ref, gain_ref):
    total = jnp.sum(in_ref[...].astype(F32), axis=0) * factor
    body = total.shape[0] - 8
    out_ref[:, 0:body, :] = jnp.broadcast_to(total[0:body].astype(BF)[None], (in_ref.shape[0], body, LANES))
    out_ref[:, body:, :] = own_ref[...] + got_ref[...]
    gain_ref[...] = total[body:]


def reduce_packets(packets, own, got, factor):
    chips, lines, _ = packets.shape
    return pl.pallas_call(
        functools.partial(reduce_kernel, factor),
        out_shape=[
            jax.ShapeDtypeStruct((chips, lines - 8 + own.shape[1], LANES), BF),
            jax.ShapeDtypeStruct((8, LANES), F32),
        ],
        compiler_params=pltpu.CompilerParams(vmem_limit_bytes=BIG_VMEM),
        cost_estimate=cost(packets.size, 4 * packets.size),
        name="reduce_packets",
    )(packets, own, got)


def node_kernel(asked_ref, packets_ref, cots_ref, out_ref, ends, rows, hots):
    devices, cap = asked_ref.shape
    nodes, width = cots_ref.shape
    blocks = width // LANES
    body = packets_ref.shape[1] - CORES * cap * blocks
    ends[...] = packets_ref[:, body:, :].astype(F32).reshape(ends.shape)
    spot = lax.broadcasted_iota(jnp.int32, (devices, nodes), 1)
    for k in range(cap):
        at = k * devices
        hots[at : at + devices, :] = one_hot(asked_ref[:, k : k + 1], spot)
        for j in range(blocks):
            rows[at : at + devices, j * LANES : (j + 1) * LANES] = ends[
                pl.ds(k * blocks + j, devices, stride=cap * blocks), :
            ].astype(BF)
    sums = dot(hots[...], rows[...], ((0,), (0,)))
    out_ref[...] = (cots_ref[...].astype(F32) + sums).astype(BF)


def node_grads(asked, packets, cots):
    devices, cap = asked.shape
    nodes, width = cots.shape
    slots = devices * cap
    return pl.pallas_call(
        node_kernel,
        out_shape=jax.ShapeDtypeStruct(cots.shape, BF),
        scratch_shapes=[
            pltpu.VMEM((slots * width // LANES, LANES), F32),
            pltpu.VMEM((slots, width), BF),
            pltpu.VMEM((slots, nodes), BF),
        ],
        compiler_params=pltpu.CompilerParams(vmem_limit_bytes=BIG_VMEM),
        cost_estimate=cost(2 * slots * cots.size, 4 * cots.size + 2 * packets.size),
        name="node_grads",
    )(asked, packets, cots)


def unpack_kernel(is_mine, core_ref, packets_ref, *refs):
    input_ref, output_ref, values, sems = refs[-4:]
    width = output_ref.shape[1]
    blocks = width // LANES
    chips = packets_ref.shape[0]
    piece = 2 * width // chips
    half = core_ref[0] if is_mine else 1 - core_ref[0]

    def copy(upper, a):
        if not upper:
            target = input_ref.at[pl.ds(a * width, width)]
        else:
            target = output_ref if a else input_ref.at[pl.ds(2 * width, width)]
        return pltpu.make_async_copy(values.at[pl.ds(a * width, width)], target, sems.at[a])

    for a in range(2):
        chunk = slice(a * (chips // 2), (a + 1) * (chips // 2))
        for j in range(blocks):
            values[a * width : (a + 1) * width, j * LANES : (j + 1) * LANES] = (
                packets_ref[chunk, j * piece : (j + 1) * piece, :].astype(F32).reshape(width, LANES)
            )

        @pl.when(half == 0)
        def _():
            copy(False, a).start()

        @pl.when(half != 0)
        def _():
            copy(True, a).start()

    for a in range(2):

        @pl.when(half == 0)
        def _():
            copy(False, a).wait()

        @pl.when(half != 0)
        def _():
            copy(True, a).wait()


def unpack(is_mine, core, packets, width, earlier=()):
    anywhere = pl.BlockSpec(memory_space=pl.ANY)
    return pl.pallas_call(
        functools.partial(unpack_kernel, is_mine),
        in_specs=[smem(), VMEM] + [anywhere] * len(earlier),
        out_specs=[anywhere] * 2,
        out_shape=[
            jax.ShapeDtypeStruct((3 * width, width), F32),
            jax.ShapeDtypeStruct((width, width), F32),
        ],
        scratch_shapes=[pltpu.VMEM((2 * width, width), F32), pltpu.SemaphoreType.DMA((2,))],
        input_output_aliases={2 + a: a for a in range(len(earlier))},
        compiler_params=pltpu.CompilerParams(vmem_limit_bytes=BIG_VMEM),
        cost_estimate=cost(packets.size, 6 * packets.size),
        name="unpack_mine" if is_mine else "unpack_other",
    )(core, packets, *earlier)


def on_device(
    edge_feats,
    node_feats,
    edge_cot,
    node_cot,
    requests,
    send_slot,
    recv_slot,
    w_input,
    w_output,
    norm_gain,
):
    chips, cores = lax.axis_size("chip"), lax.axis_size("core")
    devices = chips * cores
    both = ("chip", "core")
    cap = requests.shape[1] // devices
    edges, width = edge_feats.shape
    core = lax.axis_index("core").astype(jnp.int32).reshape(1)
    pairs = [(d, d ^ 1) for d in range(devices)]

    asked = lax.all_to_all(
        requests.reshape(devices, 1, cap), both, split_axis=0, concat_axis=0, tiled=True
    ).reshape(devices, cap)
    picked = pick_rows(asked, node_feats, node_cot).reshape(devices, -1, LANES)
    rows = lax.all_to_all(picked, both, split_axis=0, concat_axis=0, tiled=True).reshape(-1, LANES)
    pre, turned = prep_pass(edge_feats, w_input, TILE)
    d_preact, own, other, sums = edge_pass(
        core,
        send_slot,
        recv_slot,
        norm_gain.reshape(1, width),
        rows,
        w_input,
        w_output,
        pre,
        turned,
        edge_cot,
        cap,
    )
    merged = own + lax.ppermute(other, both, pairs)
    packets = lax.all_to_all(merged, "chip", split_axis=0, concat_axis=0, tiled=True)
    back_own, back_other = back_rows(core, sums, w_input, cap)
    back_got = lax.ppermute(back_other, both, pairs)
    factor = float(edges * devices) ** (-0.5)
    pieces, gain = reduce_packets(packets, back_own, back_got, factor)
    d_preact, pieces = lax.optimization_barrier((d_preact, pieces))
    mine = lax.all_to_all(pieces, "chip", split_axis=0, concat_axis=0, tiled=True)
    grad_edges = grad_pass(d_preact, w_input, edge_cot, 1024)
    grad_edges, mine = lax.optimization_barrier((grad_edges, mine))
    partner = lax.ppermute(mine, both, pairs)
    grad_nodes = node_grads(asked, mine, node_cot)
    grads = unpack(True, core, mine, width)
    grad_input, grad_output = unpack(False, core, partner, width, grads)
    return (
        grad_edges,
        grad_nodes,
        grad_input.reshape(3, width, width),
        grad_output,
        gain[0:8:2].reshape(width),
    )


def solution(mesh):
    pairs = Mesh(mesh.devices.reshape(-1, CORES), ("chip", "core"))
    rows = P(("chip", "core"), None)
    return jax.shard_map(
        on_device,
        mesh=pairs,
        in_specs=(rows,) * 7 + (P(),) * 3,
        out_specs=(rows, rows, P(), P(), P()),
        check_vma=False,
    )
```

```python
import functools

import jax
import jax.numpy as jnp
from jax import lax
from jax.experimental import pallas as pl
from jax.experimental.pallas import tpu as pltpu
from jax.sharding import Mesh, PartitionSpec as P

BF = jnp.bfloat16
F32 = jnp.float32
LANES = 128
CORES = 2
TILE = 768
PRE = F32
BIG_VMEM = 48 * 1024 * 1024

VMEM = pl.BlockSpec(memory_space=pltpu.VMEM)
ANYWHERE = pl.BlockSpec(memory_space=pl.ANY)

def dot(left, right, over=((1,), (0,))):
    return lax.dot_general(left, right, (over, ((), ())), preferred_element_type=F32)

def whole(shape):
    return pl.BlockSpec(shape, lambda *_: (0,) * len(shape))

def smem():
    return pl.BlockSpec(memory_space=pltpu.SMEM)

def cost(flops, moved):
    return pl.CostEstimate(flops=flops, bytes_accessed=moved, transcendentals=0)

def one_hot(left, right):
    return jnp.where(left == right, 1.0, 0.0).astype(BF)

def pick_kernel(asked_ref, feats_hbm, cots_hbm, out_ref, feats, cots, rows, sems):
    devices, cap = asked_ref.shape
    nodes, width = feats.shape
    blocks = width // LANES
    per = cap * 2 * blocks
    copies = [
        pltpu.make_async_copy(feats_hbm, feats, sems.at[0]),
        pltpu.make_async_copy(cots_hbm, cots, sems.at[1]),
    ]
    for copy in copies:
        copy.start()
    spot = lax.broadcasted_iota(jnp.int32, (devices, nodes), 1)
    hots = [one_hot(asked_ref[:, k : k + 1], spot) for k in range(cap)]
    for at, table in enumerate((feats, cots)):
        copies[at].wait()
        for k in range(cap):
            found = dot(hots[k], table[...])
            for j in range(blocks):
                rows[pl.ds(k * 2 * blocks + at * blocks + j, devices, stride=per), :] = found[
                    :, j * LANES : (j + 1) * LANES
                ]
    out_ref[...] = rows[...].astype(BF)

def pick_rows(asked, feats, cots):
    devices, cap = asked.shape
    width = feats.shape[1]
    total = devices * cap * 2 * width // LANES
    return pl.pallas_call(
        pick_kernel,
        in_specs=[VMEM, ANYWHERE, ANYWHERE],
        out_shape=jax.ShapeDtypeStruct((total, LANES), BF),
        scratch_shapes=[
            pltpu.VMEM(feats.shape, BF),
            pltpu.VMEM(cots.shape, BF),
            pltpu.VMEM((total, LANES), F32),
            pltpu.SemaphoreType.DMA((2,)),
        ],
        compiler_params=pltpu.CompilerParams(vmem_limit_bytes=BIG_VMEM),
        cost_estimate=cost(4 * devices * cap * feats.size, 4 * total * LANES),
        name="pick_rows",
    )(asked, feats, cots)

def slot_ids(position, chips, cap):
    half = cap * chips
    core = jnp.where(position >= half, 1, 0)
    rest = position - core * half
    k = jnp.where(rest >= chips, 1, 0) + jnp.where(rest >= 2 * chips, 1, 0)
    chip = rest - k * chips
    return chip * (CORES * cap) + core * cap + k

def prep_kernel(feats_ref, w_ref, pre_ref, turned_ref):
    feats = feats_ref[...]
    pre_ref[...] = dot(feats, w_ref[0]).astype(PRE)
    turned_ref[0] = feats.T

def prep_pass(feats, w_input, tile):
    edges, width = feats.shape
    tiles = edges // tile
    rows = pl.BlockSpec((tile, width), lambda i: (i, 0))
    return pl.pallas_call(
        prep_kernel,
        grid=(tiles,),
        in_specs=[rows, pl.BlockSpec((1, width, width), lambda i: (0, 0, 0))],
        out_specs=[rows, pl.BlockSpec((1, width, tile), lambda i: (i, 0, 0))],
        out_shape=[
            jax.ShapeDtypeStruct((edges, width), PRE),
            jax.ShapeDtypeStruct((tiles, width, tile), BF),
        ],
        compiler_params=pltpu.CompilerParams(vmem_limit_bytes=BIG_VMEM),
        cost_estimate=cost(2 * edges * width * width, 8 * feats.size),
        name="prep_pass",
    )(feats, w_input)

def grad_kernel(d_preact_ref, w_ref, cot_ref, out_ref):
    grad = dot(d_preact_ref[...], w_ref[0], ((1,), (1,)))
    out_ref[...] = (cot_ref[...].astype(F32) + grad).astype(BF)

def grad_pass(d_preact, w_input, cot, tile):
    edges, width = cot.shape
    tiles = pl.BlockSpec((tile, width), lambda i: (i, 0))
    return pl.pallas_call(
        grad_kernel,
        grid=(edges // tile,),
        in_specs=[tiles, pl.BlockSpec((1, width, width), lambda i: (0, 0, 0)), tiles],
        out_specs=tiles,
        out_shape=jax.ShapeDtypeStruct(cot.shape, BF),
        cost_estimate=cost(2 * edges * width * width, 6 * cot.size),
        name="grad_pass",
    )(d_preact, w_input, cot)

def edge_kernel(
    cap,
    core_ref,
    send_ref,
    recv_ref,
    gain_ref,
    rows_hbm,
    w_in_hbm,
    w_out_hbm,
    pre_hbm,
    turned_hbm,
    cot_hbm,
    d_preact_hbm,
    own_ref,
    other_ref,
    sums_hbm,
    rows16,
    rows32,
    w_in,
    w_out,
    pre,
    left,
    cot,
    d_preact,
    feat_tab,
    cot_tab,
    pre_tab,
    hot_rows,
    hidden,
    d_mixed,
    sums,
    sums16,
    grads,
    gain_sum,
    once,
    per_tile,
):
    tiles, _, tile = turned_hbm.shape
    slots, width = feat_tab.shape
    chips = slots // (cap * CORES)
    blocks = width // LANES
    per = cap * 2 * blocks
    groups = tile // LANES

    def span(t):
        return pl.ds(t * tile, tile)

    first = (
        pltpu.make_async_copy(rows_hbm, rows16, once.at[0]),
        pltpu.make_async_copy(w_in_hbm.at[pl.ds(1, 2)], w_in, once.at[1]),
        pltpu.make_async_copy(w_out_hbm, w_out, once.at[2]),
    )

    def load(t):
        return (
            pltpu.make_async_copy(pre_hbm.at[span(t)], pre.at[span(t)], per_tile.at[0, t]),
            pltpu.make_async_copy(cot_hbm.at[span(t)], cot.at[span(t)], per_tile.at[1, t]),
            pltpu.make_async_copy(turned_hbm.at[t], left.at[t, pl.ds(2 * slots, width)], per_tile.at[2, t]),
        )

    def leave(t):
        return pltpu.make_async_copy(d_preact.at[span(t)], d_preact_hbm.at[span(t)], per_tile.at[3, t])

    for copy in first:
        copy.start()
    for copy in load(0):
        copy.start()

    lane_ids = slot_ids(lax.broadcasted_iota(jnp.int32, (1, slots), 1), chips, cap)
    row_ids = slot_ids(lax.broadcasted_iota(jnp.int32, (slots, LANES), 0), chips, cap)

    def mark_rows(t):
        for g in range(groups):
            for at, ref in enumerate((send_ref, recv_ref)):
                upright = jnp.broadcast_to(ref[pl.ds(t * groups + g, 1), :], (LANES, LANES)).T
                for b in range(slots // LANES):
                    hot_rows[t % 2, g * LANES : (g + 1) * LANES, at * slots + b * LANES : at * slots + (b + 1) * LANES] = (
                        one_hot(upright, lane_ids[:, b * LANES : (b + 1) * LANES])
                    )

    def mark_cols(t):
        for g in range(groups):
            for at, ref in enumerate((send_ref, recv_ref)):
                left[t, at * slots : (at + 1) * slots, g * LANES : (g + 1) * LANES] = one_hot(
                    row_ids, ref[pl.ds(t * groups + g, 1), :]
                )

    sums[...] = jnp.zeros_like(sums)
    grads[3 * width : 4 * width, :] = jnp.zeros((width, width), F32)
    gain_sum[...] = jnp.zeros_like(gain_sum)
    first[0].wait()
    rows32[...] = rows16[...].astype(F32)
    for core in range(CORES):
        for k in range(cap):
            at = (core * cap + k) * chips
            for j in range(blocks):
                cols = slice(j * LANES, (j + 1) * LANES)
                begin = core * per + k * 2 * blocks + j
                feat_tab[at : at + chips, cols] = rows32[pl.ds(begin, chips, stride=CORES * per), :].astype(BF)
                cot_tab[at : at + chips, cols] = rows32[
                    pl.ds(begin + blocks, chips, stride=CORES * per), :
                ].astype(BF)
    first[1].wait()
    for t in range(1, tiles):
        for copy in load(t):
            copy.start()
    for part in range(2):
        pre_tab[part * slots : (part + 1) * slots, :] = dot(feat_tab[...], w_in[part]).astype(BF)
    first[2].wait()
    for copy in load(0):
        copy.wait()

    def gather(t):
        mark_rows(t)
        return pre[span(t), :].astype(F32) + dot(hot_rows[t % 2], pre_tab[...])

    def contract_output(t):
        grads[3 * width : 4 * width, :] += dot(hidden[t % 2], d_mixed[t % 2], ((0,), (0,)))

    def contract_input(t):
        mark_cols(t)
        sums[...] += dot(left[t], d_preact[span(t), :])

    preact = gather(0)
    for t in range(tiles):
        if t:
            contract_output(t - 1)
        logistic = 0.5 * jnp.tanh(0.5 * preact) + 0.5
        silu = preact * logistic
        rounded = silu.astype(BF)
        hidden[t % 2] = rounded
        slope = logistic + silu * (1.0 - logistic)
        mixed = dot(rounded, w_out[...])
        found = dot(hot_rows[t % 2, :, slots:], cot_tab[...])
        if t:
            contract_input(t - 1)
        center = mixed - jnp.mean(mixed, axis=1, keepdims=True)
        inverse = lax.rsqrt(jnp.mean(center * center, axis=1, keepdims=True) + 1e-5)
        normed = center * inverse
        upstream = cot[span(t), :].astype(F32) + found
        scaled = upstream * gain_ref[...]
        turned_back = (
            inverse
            * (
                scaled
                - jnp.mean(scaled, axis=1, keepdims=True)
                - normed * jnp.mean(scaled * normed, axis=1, keepdims=True)
            )
        ).astype(BF)
        gain_sum[...] += jnp.sum((upstream * normed).reshape(tile // 8, 8, width), axis=0)
        d_mixed[t % 2] = turned_back
        d_hidden = dot(turned_back, w_out[...], ((1,), (1,)))
        if t + 1 < tiles:
            for copy in load(t + 1):
                copy.wait()
            preact = gather(t + 1)
        d_preact[span(t), :] = (d_hidden * slope).astype(BF)
        leave(t).start()
    contract_output(tiles - 1)
    contract_input(tiles - 1)

    sums16[...] = sums[0 : 2 * slots, :].astype(BF)
    summed = pltpu.make_async_copy(sums16, sums_hbm, once.at[3])
    summed.start()
    grads[0:width, :] = sums[2 * slots :, :]
    for part in range(2):
        grads[(part + 1) * width : (part + 2) * width, :] = dot(
            feat_tab[...], sums16[part * slots : (part + 1) * slots, :], ((0,), (0,))
        )
    gain = jnp.sum(gain_sum[...], axis=0, keepdims=True)
    core = core_ref[0]
    piece = 2 * width // chips
    body = piece * blocks
    for target, which in ((other_ref, 1 - core), (own_ref, core)):
        begin = pl.multiple_of(which * (2 * width), 2 * width)
        for j in range(blocks):
            target[:, j * piece : (j + 1) * piece, :] = (
                grads[pl.ds(begin, 2 * width), j * LANES : (j + 1) * LANES]
                .reshape(chips, piece, LANES)
                .astype(BF)
            )
        lines = [jnp.broadcast_to(gain[:, j * LANES : (j + 1) * LANES], (2, LANES)) for j in range(blocks)]
        target[:, body:, :] = jnp.broadcast_to(jnp.concatenate(lines, axis=0)[None].astype(BF), (chips, 8, LANES))
    summed.wait()
    for t in range(tiles):
        leave(t).wait()

def edge_pass(core, send_slot, recv_slot, gain, rows, w_input, w_output, pre, turned, cot, cap):
    edges, width = cot.shape
    tiles, _, tile = turned.shape
    devices = rows.shape[0] * LANES // (cap * 2 * width)
    slots = devices * cap
    chips = devices // CORES
    packets = jax.ShapeDtypeStruct((chips, 2 * width // chips * (width // LANES) + 8, LANES), BF)
    return pl.pallas_call(
        functools.partial(edge_kernel, cap),
        in_specs=[smem()] + [VMEM] * 3 + [ANYWHERE] * 6,
        out_specs=[ANYWHERE, VMEM, VMEM, ANYWHERE],
        out_shape=[
            jax.ShapeDtypeStruct(cot.shape, BF),
            packets,
            packets,
            jax.ShapeDtypeStruct((2 * slots, width), BF),
        ],
        scratch_shapes=[
            pltpu.VMEM(rows.shape, BF),
            pltpu.VMEM(rows.shape, F32),
            pltpu.VMEM((2, width, width), BF),
            pltpu.VMEM((width, width), BF),
            pltpu.VMEM(pre.shape, pre.dtype),
            pltpu.VMEM((tiles, 2 * slots + width, tile), BF),
            pltpu.VMEM(cot.shape, BF),
            pltpu.VMEM(cot.shape, BF),
            pltpu.VMEM((slots, width), BF),
            pltpu.VMEM((slots, width), BF),
            pltpu.VMEM((2 * slots, width), BF),
            pltpu.VMEM((2, tile, 2 * slots), BF),
            pltpu.VMEM((2, tile, width), BF),
            pltpu.VMEM((2, tile, width), BF),
            pltpu.VMEM((2 * slots + width, width), F32),
            pltpu.VMEM((2 * slots, width), BF),
            pltpu.VMEM((4 * width, width), F32),
            pltpu.VMEM((8, width), F32),
            pltpu.SemaphoreType.DMA((4,)),
            pltpu.SemaphoreType.DMA((4, tiles)),
        ],
        compiler_params=pltpu.CompilerParams(vmem_limit_bytes=BIG_VMEM),
        cost_estimate=cost(16 * edges * width * width, 8 * cot.size),
        name="edge_pass",
    )(core, send_slot, recv_slot, gain, rows, w_input, w_output, pre, turned, cot)

def back_kernel(cap, core_ref, sums_ref, w_ref, own_hbm, other_ref, tail, own, sem):
    slots = sums_ref.shape[0] // 2
    width = sums_ref.shape[1]
    chips = slots // (cap * CORES)
    blocks = width // LANES
    nodes = dot(sums_ref[0:slots, :], w_ref[1], ((1,), (1,))) + dot(
        sums_ref[slots : 2 * slots, :], w_ref[2], ((1,), (1,))
    )
    core = core_ref[0]
    tail[...] = jnp.zeros_like(tail)
    for side in range(CORES):
        for k in range(cap):
            at = (side * cap + k) * chips
            for j in range(blocks):
                tail[side, pl.ds(core * (cap * blocks) + k * blocks + j, chips, stride=CORES * cap * blocks), :] = (
                    nodes[at : at + chips, j * LANES : (j + 1) * LANES]
                )
    own[...] = tail[core].astype(BF).reshape(own.shape)
    copy = pltpu.make_async_copy(own, own_hbm, sem)
    copy.start()
    other_ref[...] = tail[1 - core].astype(BF).reshape(other_ref.shape)
    copy.wait()

def back_rows(core, sums, w_input, cap):
    slots, width = sums.shape[0] // 2, sums.shape[1]
    chips = slots // (cap * CORES)
    lines = CORES * cap * width // LANES
    return pl.pallas_call(
        functools.partial(back_kernel, cap),
        in_specs=[smem(), VMEM, VMEM],
        out_specs=[ANYWHERE, VMEM],
        out_shape=[jax.ShapeDtypeStruct((chips, lines, LANES), BF)] * 2,
        scratch_shapes=[
            pltpu.VMEM((CORES, chips * lines, LANES), F32),
            pltpu.VMEM((chips, lines, LANES), BF),
            pltpu.SemaphoreType.DMA,
        ],
        compiler_params=pltpu.CompilerParams(vmem_limit_bytes=BIG_VMEM),
        cost_estimate=cost(2 * sums.size * width, 6 * sums.size),
        name="back_rows",
    )(core, sums, w_input)

def reduce_kernel(factor, in_ref, own_hbm, got_ref, out_ref, gain_ref, own, sem):
    copy = pltpu.make_async_copy(own_hbm, own, sem)
    copy.start()
    total = jnp.sum(in_ref[...].astype(F32), axis=0) * factor
    body = total.shape[0] - 8
    out_ref[:, 0:body, :] = jnp.broadcast_to(total[0:body].astype(BF)[None], (in_ref.shape[0], body, LANES))
    gain_ref[...] = jnp.concatenate([total[body + 2 * j : body + 2 * j + 1] for j in range(4)], axis=1)
    copy.wait()
    out_ref[:, body:, :] = own[...] + got_ref[...]

def reduce_packets(packets, own, got, factor):
    chips, lines, _ = packets.shape
    return pl.pallas_call(
        functools.partial(reduce_kernel, factor),
        out_shape=[
            jax.ShapeDtypeStruct((chips, lines - 8 + own.shape[1], LANES), BF),
            jax.ShapeDtypeStruct((1, 4 * LANES), F32),
        ],
        in_specs=[VMEM, ANYWHERE, VMEM],
        scratch_shapes=[pltpu.VMEM(own.shape, BF), pltpu.SemaphoreType.DMA],
        compiler_params=pltpu.CompilerParams(vmem_limit_bytes=BIG_VMEM),
        cost_estimate=cost(packets.size, 4 * packets.size),
        name="reduce_packets",
    )(packets, own, got)

def node_kernel(asked_ref, packets_ref, cots_ref, out_ref, ends, rows, hots):
    devices, cap = asked_ref.shape
    nodes, width = cots_ref.shape
    blocks = width // LANES
    body = packets_ref.shape[1] - CORES * cap * blocks
    ends[...] = packets_ref[:, body:, :].astype(F32).reshape(ends.shape)
    spot = lax.broadcasted_iota(jnp.int32, (devices, nodes), 1)
    for k in range(cap):
        at = k * devices
        hots[at : at + devices, :] = one_hot(asked_ref[:, k : k + 1], spot)
        for j in range(blocks):
            rows[at : at + devices, j * LANES : (j + 1) * LANES] = ends[
                pl.ds(k * blocks + j, devices, stride=cap * blocks), :
            ].astype(BF)
    sums = dot(hots[...], rows[...], ((0,), (0,)))
    out_ref[...] = (cots_ref[...].astype(F32) + sums).astype(BF)

def node_grads(asked, packets, cots):
    devices, cap = asked.shape
    nodes, width = cots.shape
    slots = devices * cap
    return pl.pallas_call(
        node_kernel,
        out_shape=jax.ShapeDtypeStruct(cots.shape, BF),
        scratch_shapes=[
            pltpu.VMEM((slots * width // LANES, LANES), F32),
            pltpu.VMEM((slots, width), BF),
            pltpu.VMEM((slots, nodes), BF),
        ],
        compiler_params=pltpu.CompilerParams(vmem_limit_bytes=BIG_VMEM),
        cost_estimate=cost(2 * slots * cots.size, 4 * cots.size + 2 * packets.size),
        name="node_grads",
    )(asked, packets, cots)

def unpack_kernel(is_mine, core_ref, packets_ref, *refs):
    input_ref, output_ref, values, sems = refs[-4:]
    width = output_ref.shape[1]
    blocks = width // LANES
    chips = packets_ref.shape[0]
    piece = 2 * width // chips
    half = core_ref[0] if is_mine else 1 - core_ref[0]

    def copy(upper, a):
        if not upper:
            target = input_ref.at[pl.ds(a * width, width)]
        else:
            target = output_ref if a else input_ref.at[pl.ds(2 * width, width)]
        return pltpu.make_async_copy(values.at[pl.ds(a * width, width)], target, sems.at[a])

    for a in range(2):
        chunk = slice(a * (chips // 2), (a + 1) * (chips // 2))
        for j in range(blocks):
            values[a * width : (a + 1) * width, j * LANES : (j + 1) * LANES] = (
                packets_ref[chunk, j * piece : (j + 1) * piece, :].astype(F32).reshape(width, LANES)
            )

        @pl.when(half == 0)
        def _():
            copy(False, a).start()

        @pl.when(half != 0)
        def _():
            copy(True, a).start()

    for a in range(2):

        @pl.when(half == 0)
        def _():
            copy(False, a).wait()

        @pl.when(half != 0)
        def _():
            copy(True, a).wait()

def unpack(is_mine, core, packets, width, earlier=()):
    return pl.pallas_call(
        functools.partial(unpack_kernel, is_mine),
        in_specs=[smem(), VMEM] + [ANYWHERE] * len(earlier),
        out_specs=[ANYWHERE] * 2,
        out_shape=[
            jax.ShapeDtypeStruct((3 * width, width), F32),
            jax.ShapeDtypeStruct((width, width), F32),
        ],
        scratch_shapes=[pltpu.VMEM((2 * width, width), F32), pltpu.SemaphoreType.DMA((2,))],
        input_output_aliases={2 + a: a for a in range(len(earlier))},
        compiler_params=pltpu.CompilerParams(vmem_limit_bytes=BIG_VMEM),
        cost_estimate=cost(packets.size, 6 * packets.size),
        name="unpack_mine" if is_mine else "unpack_other",
    )(core, packets, *earlier)

def on_device(
    edge_feats,
    node_feats,
    edge_cot,
    node_cot,
    requests,
    send_slot,
    recv_slot,
    w_input,
    w_output,
    norm_gain,
):
    chips, cores = lax.axis_size("chip"), lax.axis_size("core")
    devices = chips * cores
    both = ("chip", "core")
    cap = requests.shape[1] // devices
    edges, width = edge_feats.shape
    core = lax.axis_index("core").astype(jnp.int32).reshape(1)
    pairs = [(d, d ^ 1) for d in range(devices)]

    asked = lax.all_to_all(
        requests.reshape(devices, 1, cap), both, split_axis=0, concat_axis=0, tiled=True
    ).reshape(devices, cap)
    picked = pick_rows(asked, node_feats, node_cot).reshape(devices, -1, LANES)
    rows = lax.all_to_all(picked, both, split_axis=0, concat_axis=0, tiled=True).reshape(-1, LANES)
    pre, turned = prep_pass(edge_feats, w_input, TILE)
    d_preact, own, other, sums = edge_pass(
        core,
        send_slot,
        recv_slot,
        norm_gain.reshape(1, width),
        rows,
        w_input,
        w_output,
        pre,
        turned,
        edge_cot,
        cap,
    )
    merged = own + lax.ppermute(other, both, pairs)
    packets = lax.all_to_all(merged, "chip", split_axis=0, concat_axis=0, tiled=True)
    back_own, back_other = back_rows(core, sums, w_input, cap)
    back_got = lax.ppermute(back_other, both, pairs)
    factor = float(edges * devices) ** (-0.5)
    pieces, gain = reduce_packets(packets, back_own, back_got, factor)
    d_preact, pieces = lax.optimization_barrier((d_preact, pieces))
    mine = lax.all_to_all(pieces, "chip", split_axis=0, concat_axis=0, tiled=True)
    grad_edges = grad_pass(d_preact, w_input, edge_cot, 1024)
    grad_edges, mine = lax.optimization_barrier((grad_edges, mine))
    partner = lax.ppermute(mine, both, pairs)
    grad_nodes = node_grads(asked, mine, node_cot)
    grads = unpack(True, core, mine, width)
    grad_input, grad_output = unpack(False, core, partner, width, grads)
    return (
        grad_edges,
        grad_nodes,
        grad_input.reshape(3, width, width),
        grad_output,
        gain.reshape(width),
    )

def solution(mesh):
    pairs = Mesh(mesh.devices.reshape(-1, CORES), ("chip", "core"))
    rows = P(("chip", "core"), None)
    return jax.shard_map(
        on_device,
        mesh=pairs,
        in_specs=(rows,) * 7 + (P(),) * 3,
        out_specs=(rows, rows, P(), P(), P()),
        check_vma=False,
    )
```

```python
import functools

import jax
import jax.numpy as jnp
from jax import lax
from jax.experimental import pallas as pl
from jax.experimental.pallas import tpu as pltpu
from jax.sharding import Mesh, PartitionSpec as P

BF = jnp.bfloat16
F32 = jnp.float32
LANES = 128
CORES = 2
TILE = 768
CHUNKS = 2
PRE = F32
BIG_VMEM = 48 * 1024 * 1024

VMEM = pl.BlockSpec(memory_space=pltpu.VMEM)
ANYWHERE = pl.BlockSpec(memory_space=pl.ANY)
HBM = pl.BlockSpec(memory_space=pltpu.HBM)

def dot(left, right, over=((1,), (0,))):
    return lax.dot_general(left, right, (over, ((), ())), preferred_element_type=F32)

def in_hbm(array):
    return pltpu.with_memory_space_constraint(array, pltpu.HBM)

def smem():
    return pl.BlockSpec(memory_space=pltpu.SMEM)

def cost(flops, moved):
    return pl.CostEstimate(flops=flops, bytes_accessed=moved, transcendentals=0)

def one_hot(left, right):
    return jnp.where(left == right, 1.0, 0.0).astype(BF)

def pick_kernel(asked_ref, feats_hbm, cots_hbm, out_ref, feats, cots, rows, sems):
    devices, cap = asked_ref.shape
    nodes, width = feats.shape
    blocks = width // LANES
    per = cap * 2 * blocks
    copies = [
        pltpu.make_async_copy(feats_hbm, feats, sems.at[0]),
        pltpu.make_async_copy(cots_hbm, cots, sems.at[1]),
    ]
    for copy in copies:
        copy.start()
    spot = lax.broadcasted_iota(jnp.int32, (devices, nodes), 1)
    hots = [one_hot(asked_ref[:, k : k + 1], spot) for k in range(cap)]
    for at, table in enumerate((feats, cots)):
        copies[at].wait()
        for k in range(cap):
            found = dot(hots[k], table[...])
            for j in range(blocks):
                rows[pl.ds(k * 2 * blocks + at * blocks + j, devices, stride=per), :] = found[
                    :, j * LANES : (j + 1) * LANES
                ]
    out_ref[...] = rows[...].astype(BF)

def pick_rows(asked, feats, cots):
    devices, cap = asked.shape
    width = feats.shape[1]
    total = devices * cap * 2 * width // LANES
    return pl.pallas_call(
        pick_kernel,
        in_specs=[VMEM, HBM, HBM],
        out_shape=jax.ShapeDtypeStruct((total, LANES), BF),
        scratch_shapes=[
            pltpu.VMEM(feats.shape, BF),
            pltpu.VMEM(cots.shape, BF),
            pltpu.VMEM((total, LANES), F32),
            pltpu.SemaphoreType.DMA((2,)),
        ],
        compiler_params=pltpu.CompilerParams(vmem_limit_bytes=BIG_VMEM),
        cost_estimate=cost(4 * devices * cap * feats.size, 4 * total * LANES),
        name="pick_rows",
    )(asked, in_hbm(feats), in_hbm(cots))

def slot_ids(position, chips, cap):
    half = cap * chips
    core = jnp.where(position >= half, 1, 0)
    rest = position - core * half
    k = jnp.where(rest >= chips, 1, 0) + jnp.where(rest >= 2 * chips, 1, 0)
    chip = rest - k * chips
    return chip * (CORES * cap) + core * cap + k

def prep_kernel(feats_ref, w_ref, pre_ref, turned_ref):
    feats = feats_ref[...]
    pre_ref[...] = dot(feats, w_ref[0]).astype(PRE)
    turned_ref[0] = feats.T

def prep_pass(feats, w_input, tile):
    edges, width = feats.shape
    tiles = edges // tile
    rows = pl.BlockSpec((tile, width), lambda i: (i, 0))
    return pl.pallas_call(
        prep_kernel,
        grid=(tiles,),
        in_specs=[rows, pl.BlockSpec((1, width, width), lambda i: (0, 0, 0))],
        out_specs=[rows, pl.BlockSpec((1, width, tile), lambda i: (i, 0, 0))],
        out_shape=[
            jax.ShapeDtypeStruct((edges, width), PRE),
            jax.ShapeDtypeStruct((tiles, width, tile), BF),
        ],
        compiler_params=pltpu.CompilerParams(vmem_limit_bytes=BIG_VMEM),
        cost_estimate=cost(2 * edges * width * width, 8 * feats.size),
        name="prep_pass",
    )(feats, w_input)

def grad_kernel(d_preact_ref, w_ref, cot_ref, out_ref):
    grad = dot(d_preact_ref[...], w_ref[0], ((1,), (1,)))
    out_ref[...] = (cot_ref[...].astype(F32) + grad).astype(BF)

def grad_pass(d_preact, w_input, cot, tile):
    edges, width = cot.shape
    tiles = pl.BlockSpec((tile, width), lambda i: (i, 0))
    return pl.pallas_call(
        grad_kernel,
        grid=(edges // tile,),
        in_specs=[tiles, pl.BlockSpec((1, width, width), lambda i: (0, 0, 0)), tiles],
        out_specs=tiles,
        out_shape=jax.ShapeDtypeStruct(cot.shape, BF),
        cost_estimate=cost(2 * edges * width * width, 6 * cot.size),
        name="grad_pass",
    )(in_hbm(d_preact), w_input, in_hbm(cot))

def edge_kernel(
    cap,
    core_ref,
    send_ref,
    recv_ref,
    gain_ref,
    rows_ref,
    w_in,
    w_out,
    pre_hbm,
    turned_hbm,
    cot_hbm,
    d_preact_hbm,
    own_ref,
    other_ref,
    sums_ref,
    rows32,
    pre,
    left,
    cot,
    d_preact,
    feat_tab,
    cot_tab,
    pre_tab,
    hot_rows,
    hidden,
    d_mixed,
    sums,
    grads,
    gain_sum,
    per_tile,
):
    tiles, _, tile = turned_hbm.shape
    slots, width = feat_tab.shape
    chips = slots // (cap * CORES)
    blocks = width // LANES
    per = cap * 2 * blocks
    groups = tile // LANES

    def span(t):
        return pl.ds(t * tile, tile)

    def load(t):
        return (
            pltpu.make_async_copy(pre_hbm.at[span(t)], pre.at[span(t)], per_tile.at[0, t]),
            pltpu.make_async_copy(cot_hbm.at[span(t)], cot.at[span(t)], per_tile.at[1, t]),
            pltpu.make_async_copy(turned_hbm.at[t], left.at[t, pl.ds(2 * slots, width)], per_tile.at[2, t]),
        )

    def leave(t):
        return pltpu.make_async_copy(d_preact.at[span(t)], d_preact_hbm.at[span(t)], per_tile.at[3, t])

    for t in range(tiles):
        for copy in load(t):
            copy.start()

    lane_ids = slot_ids(lax.broadcasted_iota(jnp.int32, (1, slots), 1), chips, cap)
    row_ids = slot_ids(lax.broadcasted_iota(jnp.int32, (slots, LANES), 0), chips, cap)

    def mark_rows(t):
        for g in range(groups):
            for at, ref in enumerate((send_ref, recv_ref)):
                upright = jnp.broadcast_to(ref[pl.ds(t * groups + g, 1), :], (LANES, LANES)).T
                for b in range(slots // LANES):
                    hot_rows[t % 2, g * LANES : (g + 1) * LANES, at * slots + b * LANES : at * slots + (b + 1) * LANES] = (
                        one_hot(upright, lane_ids[:, b * LANES : (b + 1) * LANES])
                    )

    def mark_cols(t):
        for g in range(groups):
            for at, ref in enumerate((send_ref, recv_ref)):
                left[t, at * slots : (at + 1) * slots, g * LANES : (g + 1) * LANES] = one_hot(
                    row_ids, ref[pl.ds(t * groups + g, 1), :]
                )

    sums[...] = jnp.zeros_like(sums)
    grads[3 * width : 4 * width, :] = jnp.zeros((width, width), F32)
    gain_sum[...] = jnp.zeros_like(gain_sum)
    rows32[...] = rows_ref[...].astype(F32)
    for core in range(CORES):
        for k in range(cap):
            at = (core * cap + k) * chips
            for j in range(blocks):
                cols = slice(j * LANES, (j + 1) * LANES)
                begin = core * per + k * 2 * blocks + j
                feat_tab[at : at + chips, cols] = rows32[pl.ds(begin, chips, stride=CORES * per), :].astype(BF)
                cot_tab[at : at + chips, cols] = rows32[
                    pl.ds(begin + blocks, chips, stride=CORES * per), :
                ].astype(BF)
    for part in range(2):
        pre_tab[part * slots : (part + 1) * slots, :] = dot(feat_tab[...], w_in[part + 1]).astype(BF)
    for copy in load(0):
        copy.wait()

    def gather(t):
        mark_rows(t)
        return pre[span(t), :].astype(F32) + dot(hot_rows[t % 2], pre_tab[...])

    def contract_output(t):
        grads[3 * width : 4 * width, :] += dot(hidden[t % 2], d_mixed[t % 2], ((0,), (0,)))

    def contract_input(t, c):
        lines = (2 * slots + width) // CHUNKS
        part = slice(c * lines, (c + 1) * lines)
        sums[part, :] += dot(left[t, part, :], d_preact[span(t), :])

    preact = gather(0)
    for t in range(tiles):
        if t:
            contract_output(t - 1)
        logistic = 0.5 * jnp.tanh(0.5 * preact) + 0.5
        silu = preact * logistic
        rounded = silu.astype(BF)
        hidden[t % 2] = rounded
        slope = logistic + silu * (1.0 - logistic)
        mixed = dot(rounded, w_out[...])
        found = dot(hot_rows[t % 2, :, slots:], cot_tab[...])
        if t:
            mark_cols(t - 1)
        for c in range(CHUNKS):
            if t:
                contract_input(t - 1, c)
            part = slice(c * (tile // CHUNKS), (c + 1) * (tile // CHUNKS))
            center = mixed[part] - jnp.mean(mixed[part], axis=1, keepdims=True)
            inverse = lax.rsqrt(jnp.mean(center * center, axis=1, keepdims=True) + 1e-5)
            normed = center * inverse
            scaled = (cot[pl.ds(t * tile + part.start, tile // CHUNKS), :].astype(F32) + found[part]) * gain_ref[...]
            product = scaled * normed
            d_mixed[t % 2, part, :] = (
                inverse
                * (
                    scaled
                    - jnp.mean(scaled, axis=1, keepdims=True)
                    - normed * jnp.mean(product, axis=1, keepdims=True)
                )
            ).astype(BF)
            gain_sum[...] += jnp.sum(product.reshape(-1, 8, width), axis=0)
        d_hidden = dot(d_mixed[t % 2], w_out[...], ((1,), (1,)))
        if t + 1 < tiles:
            for copy in load(t + 1):
                copy.wait()
            preact = gather(t + 1)
        d_preact[span(t), :] = (d_hidden * slope).astype(BF)
        leave(t).start()
    contract_output(tiles - 1)
    mark_cols(tiles - 1)
    for c in range(CHUNKS):
        contract_input(tiles - 1, c)

    sums_ref[...] = sums[0 : 2 * slots, :].astype(BF)
    grads[0:width, :] = sums[2 * slots :, :]
    for part in range(2):
        grads[(part + 1) * width : (part + 2) * width, :] = dot(
            feat_tab[...], sums_ref[part * slots : (part + 1) * slots, :], ((0,), (0,))
        )
    gain = jnp.sum(gain_sum[...], axis=0, keepdims=True) / gain_ref[...]
    core = core_ref[0]
    piece = 2 * width // chips
    body = piece * blocks
    for target, which in ((other_ref, 1 - core), (own_ref, core)):
        begin = pl.multiple_of(which * (2 * width), 2 * width)
        for j in range(blocks):
            target[:, j * piece : (j + 1) * piece, :] = (
                grads[pl.ds(begin, 2 * width), j * LANES : (j + 1) * LANES]
                .reshape(chips, piece, LANES)
                .astype(BF)
            )
        lines = [jnp.broadcast_to(gain[:, j * LANES : (j + 1) * LANES], (2, LANES)) for j in range(blocks)]
        target[:, body:, :] = jnp.broadcast_to(jnp.concatenate(lines, axis=0)[None].astype(BF), (chips, 8, LANES))
    for t in range(tiles):
        leave(t).wait()

def edge_pass(core, send_slot, recv_slot, gain, rows, w_input, w_output, pre, turned, cot, cap):
    edges, width = cot.shape
    tiles, _, tile = turned.shape
    devices = rows.shape[0] * LANES // (cap * 2 * width)
    slots = devices * cap
    chips = devices // CORES
    packets = jax.ShapeDtypeStruct((chips, 2 * width // chips * (width // LANES) + 8, LANES), BF)
    return pl.pallas_call(
        functools.partial(edge_kernel, cap),
        in_specs=[smem()] + [VMEM] * 6 + [HBM] * 3,
        out_specs=[HBM, VMEM, VMEM, VMEM],
        out_shape=[
            jax.ShapeDtypeStruct(cot.shape, BF),
            packets,
            packets,
            jax.ShapeDtypeStruct((2 * slots, width), BF),
        ],
        scratch_shapes=[
            pltpu.VMEM(rows.shape, F32),
            pltpu.VMEM(pre.shape, pre.dtype),
            pltpu.VMEM((tiles, 2 * slots + width, tile), BF),
            pltpu.VMEM(cot.shape, BF),
            pltpu.VMEM(cot.shape, BF),
            pltpu.VMEM((slots, width), BF),
            pltpu.VMEM((slots, width), BF),
            pltpu.VMEM((2 * slots, width), BF),
            pltpu.VMEM((2, tile, 2 * slots), BF),
            pltpu.VMEM((2, tile, width), BF),
            pltpu.VMEM((2, tile, width), BF),
            pltpu.VMEM((2 * slots + width, width), F32),
            pltpu.VMEM((4 * width, width), F32),
            pltpu.VMEM((8, width), F32),
            pltpu.SemaphoreType.DMA((4, tiles)),
        ],
        compiler_params=pltpu.CompilerParams(vmem_limit_bytes=BIG_VMEM),
        cost_estimate=cost(16 * edges * width * width, 8 * cot.size),
        name="edge_pass",
    )(core, send_slot, recv_slot, gain, rows, w_input, w_output, in_hbm(pre), in_hbm(turned), in_hbm(cot))

def back_kernel(cap, core_ref, sums_ref, w_ref, own_hbm, other_ref, tail, own, sem):
    slots = sums_ref.shape[0] // 2
    width = sums_ref.shape[1]
    chips = slots // (cap * CORES)
    blocks = width // LANES
    nodes = dot(sums_ref[0:slots, :], w_ref[1], ((1,), (1,))) + dot(
        sums_ref[slots : 2 * slots, :], w_ref[2], ((1,), (1,))
    )
    core = core_ref[0]
    tail[...] = jnp.zeros_like(tail)
    for side in range(CORES):
        for k in range(cap):
            at = (side * cap + k) * chips
            for j in range(blocks):
                tail[side, pl.ds(core * (cap * blocks) + k * blocks + j, chips, stride=CORES * cap * blocks), :] = (
                    nodes[at : at + chips, j * LANES : (j + 1) * LANES]
                )
    own[...] = tail[core].astype(BF).reshape(own.shape)
    copy = pltpu.make_async_copy(own, own_hbm, sem)
    copy.start()
    other_ref[...] = tail[1 - core].astype(BF).reshape(other_ref.shape)
    copy.wait()

def back_rows(core, sums, w_input, cap):
    slots, width = sums.shape[0] // 2, sums.shape[1]
    chips = slots // (cap * CORES)
    lines = CORES * cap * width // LANES
    return pl.pallas_call(
        functools.partial(back_kernel, cap),
        in_specs=[smem(), VMEM, VMEM],
        out_specs=[ANYWHERE, VMEM],
        out_shape=[jax.ShapeDtypeStruct((chips, lines, LANES), BF)] * 2,
        scratch_shapes=[
            pltpu.VMEM((CORES, chips * lines, LANES), F32),
            pltpu.VMEM((chips, lines, LANES), BF),
            pltpu.SemaphoreType.DMA,
        ],
        compiler_params=pltpu.CompilerParams(vmem_limit_bytes=BIG_VMEM),
        cost_estimate=cost(2 * sums.size * width, 6 * sums.size),
        name="back_rows",
    )(core, sums, w_input)

def reduce_kernel(factor, in_ref, own_hbm, got_ref, out_ref, gain_ref, own, sem):
    copy = pltpu.make_async_copy(own_hbm, own, sem)
    copy.start()
    total = jnp.sum(in_ref[...].astype(F32), axis=0) * factor
    body = total.shape[0] - 8
    out_ref[:, 0:body, :] = jnp.broadcast_to(total[0:body].astype(BF)[None], (in_ref.shape[0], body, LANES))
    gain_ref[...] = jnp.concatenate([total[body + 2 * j : body + 2 * j + 1] for j in range(4)], axis=1)
    copy.wait()
    out_ref[:, body:, :] = own[...] + got_ref[...]

def reduce_packets(packets, own, got, factor):
    chips, lines, _ = packets.shape
    return pl.pallas_call(
        functools.partial(reduce_kernel, factor),
        out_shape=[
            jax.ShapeDtypeStruct((chips, lines - 8 + own.shape[1], LANES), BF),
            jax.ShapeDtypeStruct((1, 4 * LANES), F32),
        ],
        in_specs=[VMEM, ANYWHERE, VMEM],
        scratch_shapes=[pltpu.VMEM(own.shape, BF), pltpu.SemaphoreType.DMA],
        compiler_params=pltpu.CompilerParams(vmem_limit_bytes=BIG_VMEM),
        cost_estimate=cost(packets.size, 4 * packets.size),
        name="reduce_packets",
    )(packets, in_hbm(own), got)

def node_kernel(asked_ref, packets_ref, cots_ref, out_ref, ends, rows, hots):
    devices, cap = asked_ref.shape
    nodes, width = cots_ref.shape
    blocks = width // LANES
    body = packets_ref.shape[1] - CORES * cap * blocks
    ends[...] = packets_ref[:, body:, :].astype(F32).reshape(ends.shape)
    spot = lax.broadcasted_iota(jnp.int32, (devices, nodes), 1)
    for k in range(cap):
        at = k * devices
        hots[at : at + devices, :] = one_hot(asked_ref[:, k : k + 1], spot)
        for j in range(blocks):
            rows[at : at + devices, j * LANES : (j + 1) * LANES] = ends[
                pl.ds(k * blocks + j, devices, stride=cap * blocks), :
            ].astype(BF)
    sums = dot(hots[...], rows[...], ((0,), (0,)))
    out_ref[...] = (cots_ref[...].astype(F32) + sums).astype(BF)

def node_grads(asked, packets, cots):
    devices, cap = asked.shape
    nodes, width = cots.shape
    slots = devices * cap
    return pl.pallas_call(
        node_kernel,
        out_shape=jax.ShapeDtypeStruct(cots.shape, BF),
        scratch_shapes=[
            pltpu.VMEM((slots * width // LANES, LANES), F32),
            pltpu.VMEM((slots, width), BF),
            pltpu.VMEM((slots, nodes), BF),
        ],
        compiler_params=pltpu.CompilerParams(vmem_limit_bytes=BIG_VMEM),
        cost_estimate=cost(2 * slots * cots.size, 4 * cots.size + 2 * packets.size),
        name="node_grads",
    )(asked, packets, cots)

def unpack_kernel(is_mine, core_ref, packets_ref, *refs):
    input_ref, output_ref, values, sems = refs[-4:]
    width = output_ref.shape[1]
    blocks = width // LANES
    chips = packets_ref.shape[0]
    piece = 2 * width // chips
    half = core_ref[0] if is_mine else 1 - core_ref[0]

    def copy(upper, a):
        if not upper:
            target = input_ref.at[pl.ds(a * width, width)]
        else:
            target = output_ref if a else input_ref.at[pl.ds(2 * width, width)]
        return pltpu.make_async_copy(values.at[pl.ds(a * width, width)], target, sems.at[a])

    for a in range(2):
        chunk = slice(a * (chips // 2), (a + 1) * (chips // 2))
        for j in range(blocks):
            values[a * width : (a + 1) * width, j * LANES : (j + 1) * LANES] = (
                packets_ref[chunk, j * piece : (j + 1) * piece, :].astype(F32).reshape(width, LANES)
            )

        @pl.when(half == 0)
        def _():
            copy(False, a).start()

        @pl.when(half != 0)
        def _():
            copy(True, a).start()

    for a in range(2):

        @pl.when(half == 0)
        def _():
            copy(False, a).wait()

        @pl.when(half != 0)
        def _():
            copy(True, a).wait()

def unpack(is_mine, core, packets, width, earlier=()):
    return pl.pallas_call(
        functools.partial(unpack_kernel, is_mine),
        in_specs=[smem(), VMEM] + [ANYWHERE] * len(earlier),
        out_specs=[ANYWHERE] * 2,
        out_shape=[
            jax.ShapeDtypeStruct((3 * width, width), F32),
            jax.ShapeDtypeStruct((width, width), F32),
        ],
        scratch_shapes=[pltpu.VMEM((2 * width, width), F32), pltpu.SemaphoreType.DMA((2,))],
        input_output_aliases={2 + a: a for a in range(len(earlier))},
        compiler_params=pltpu.CompilerParams(vmem_limit_bytes=BIG_VMEM),
        cost_estimate=cost(packets.size, 6 * packets.size),
        name="unpack_mine" if is_mine else "unpack_other",
    )(core, packets, *earlier)

def on_device(
    edge_feats,
    node_feats,
    edge_cot,
    node_cot,
    requests,
    send_slot,
    recv_slot,
    w_input,
    w_output,
    norm_gain,
):
    chips, cores = lax.axis_size("chip"), lax.axis_size("core")
    devices = chips * cores
    both = ("chip", "core")
    cap = requests.shape[1] // devices
    edges, width = edge_feats.shape
    core = lax.axis_index("core").astype(jnp.int32).reshape(1)
    pairs = [(d, d ^ 1) for d in range(devices)]

    asked = lax.all_to_all(
        requests.reshape(devices, 1, cap), both, split_axis=0, concat_axis=0, tiled=True
    ).reshape(devices, cap)
    picked = pick_rows(asked, node_feats, node_cot).reshape(devices, -1, LANES)
    rows = lax.all_to_all(picked, both, split_axis=0, concat_axis=0, tiled=True).reshape(-1, LANES)
    pre, turned = prep_pass(edge_feats, w_input, TILE)
    d_preact, own, other, sums = edge_pass(
        core,
        send_slot,
        recv_slot,
        norm_gain.reshape(1, width),
        rows,
        w_input,
        w_output,
        pre,
        turned,
        edge_cot,
        cap,
    )
    got = lax.ppermute(other, both, pairs)
    back_own, back_other = back_rows(core, sums, w_input, cap)
    got, back_own, back_other = lax.optimization_barrier((got, back_own, back_other))
    packets = lax.all_to_all(own + got, "chip", split_axis=0, concat_axis=0, tiled=True)
    back_got = lax.ppermute(back_other, both, pairs)
    factor = float(edges * devices) ** (-0.5)
    pieces, gain = reduce_packets(packets, back_own, back_got, factor)
    d_preact, pieces = lax.optimization_barrier((d_preact, pieces))
    mine = lax.all_to_all(pieces, "chip", split_axis=0, concat_axis=0, tiled=True)
    grad_edges = grad_pass(d_preact, w_input, edge_cot, 1024)
    grad_edges, mine = lax.optimization_barrier((grad_edges, mine))
    partner = lax.ppermute(mine, both, pairs)
    grad_nodes = node_grads(asked, mine, node_cot)
    grads = unpack(True, core, mine, width)
    grad_input, grad_output = unpack(False, core, partner, width, grads)
    return (
        grad_edges,
        grad_nodes,
        grad_input.reshape(3, width, width),
        grad_output,
        gain.reshape(width),
    )

def solution(mesh):
    pairs = Mesh(mesh.devices.reshape(-1, CORES), ("chip", "core"))
    rows = P(("chip", "core"), None)
    return jax.shard_map(
        on_device,
        mesh=pairs,
        in_specs=(rows,) * 7 + (P(),) * 3,
        out_specs=(rows, rows, P(), P(), P()),
        check_vma=False,
    )
```

```python
import functools

import jax
import jax.numpy as jnp
from jax import lax
from jax.experimental import pallas as pl
from jax.experimental.pallas import tpu as pltpu
from jax.sharding import Mesh, PartitionSpec as P

BF = jnp.bfloat16
F32 = jnp.float32
LANES = 128
CORES = 2
TILE = 768
CHUNKS = 2
PRE = F32
BIG_VMEM = 48 * 1024 * 1024

VMEM = pl.BlockSpec(memory_space=pltpu.VMEM)
ANYWHERE = pl.BlockSpec(memory_space=pl.ANY)
HBM = pl.BlockSpec(memory_space=pltpu.HBM)

def dot(left, right, over=((1,), (0,))):
    return lax.dot_general(left, right, (over, ((), ())), preferred_element_type=F32)

def in_hbm(array):
    return pltpu.with_memory_space_constraint(array, pltpu.HBM)

def smem():
    return pl.BlockSpec(memory_space=pltpu.SMEM)

def cost(flops, moved):
    return pl.CostEstimate(flops=flops, bytes_accessed=moved, transcendentals=0)

def one_hot(left, right):
    return jnp.where(left == right, 1.0, 0.0).astype(BF)

def pick_kernel(asked_ref, feats_hbm, cots_hbm, out_ref, feats, cots, rows, sems):
    devices, cap = asked_ref.shape
    nodes, width = feats.shape
    blocks = width // LANES
    per = cap * 2 * blocks
    copies = [
        pltpu.make_async_copy(feats_hbm, feats, sems.at[0]),
        pltpu.make_async_copy(cots_hbm, cots, sems.at[1]),
    ]
    for copy in copies:
        copy.start()
    spot = lax.broadcasted_iota(jnp.int32, (devices, nodes), 1)
    hots = [one_hot(asked_ref[:, k : k + 1], spot) for k in range(cap)]
    for at, table in enumerate((feats, cots)):
        copies[at].wait()
        for k in range(cap):
            found = dot(hots[k], table[...])
            for j in range(blocks):
                rows[pl.ds(k * 2 * blocks + at * blocks + j, devices, stride=per), :] = found[
                    :, j * LANES : (j + 1) * LANES
                ]
    out_ref[...] = rows[...].astype(BF)

def pick_rows(asked, feats, cots):
    devices, cap = asked.shape
    width = feats.shape[1]
    total = devices * cap * 2 * width // LANES
    return pl.pallas_call(
        pick_kernel,
        in_specs=[VMEM, HBM, HBM],
        out_specs=VMEM,
        out_shape=jax.ShapeDtypeStruct((total, LANES), BF),
        scratch_shapes=[
            pltpu.VMEM(feats.shape, BF),
            pltpu.VMEM(cots.shape, BF),
            pltpu.VMEM((total, LANES), F32),
            pltpu.SemaphoreType.DMA((2,)),
        ],
        compiler_params=pltpu.CompilerParams(vmem_limit_bytes=BIG_VMEM),
        cost_estimate=cost(4 * devices * cap * feats.size, 4 * total * LANES),
        name="pick_rows",
    )(asked, in_hbm(feats), in_hbm(cots))

def slot_ids(position, chips, cap):
    half = cap * chips
    core = jnp.where(position >= half, 1, 0)
    rest = position - core * half
    k = jnp.where(rest >= chips, 1, 0) + jnp.where(rest >= 2 * chips, 1, 0)
    chip = rest - k * chips
    return chip * (CORES * cap) + core * cap + k

def prep_kernel(feats_ref, w_ref, pre_ref, turned_ref):
    feats = feats_ref[...]
    pre_ref[...] = dot(feats, w_ref[0]).astype(PRE)
    turned_ref[0] = feats.T

def prep_pass(feats, w_input, tile):
    edges, width = feats.shape
    tiles = edges // tile
    rows = pl.BlockSpec((tile, width), lambda i: (i, 0))
    return pl.pallas_call(
        prep_kernel,
        grid=(tiles,),
        in_specs=[rows, pl.BlockSpec((1, width, width), lambda i: (0, 0, 0))],
        out_specs=[rows, pl.BlockSpec((1, width, tile), lambda i: (i, 0, 0))],
        out_shape=[
            jax.ShapeDtypeStruct((edges, width), PRE),
            jax.ShapeDtypeStruct((tiles, width, tile), BF),
        ],
        compiler_params=pltpu.CompilerParams(vmem_limit_bytes=BIG_VMEM),
        cost_estimate=cost(2 * edges * width * width, 8 * feats.size),
        name="prep_pass",
    )(feats, w_input)

def grad_kernel(d_preact_ref, w_ref, cot_ref, out_ref):
    grad = dot(d_preact_ref[...], w_ref[0], ((1,), (1,)))
    out_ref[...] = (cot_ref[...].astype(F32) + grad).astype(BF)

def grad_pass(d_preact, w_input, cot, tile):
    edges, width = cot.shape
    tiles = pl.BlockSpec((tile, width), lambda i: (i, 0))
    return pl.pallas_call(
        grad_kernel,
        grid=(edges // tile,),
        in_specs=[tiles, pl.BlockSpec((1, width, width), lambda i: (0, 0, 0)), tiles],
        out_specs=tiles,
        out_shape=jax.ShapeDtypeStruct(cot.shape, BF),
        cost_estimate=cost(2 * edges * width * width, 6 * cot.size),
        name="grad_pass",
    )(in_hbm(d_preact), w_input, in_hbm(cot))

def edge_kernel(
    cap,
    core_ref,
    send_ref,
    recv_ref,
    gain_ref,
    rows_ref,
    w_in,
    w_out,
    pre_hbm,
    turned_hbm,
    cot_hbm,
    d_preact_hbm,
    own_ref,
    other_ref,
    sums_ref,
    rows32,
    pre,
    left,
    cot,
    d_preact,
    feat_tab,
    cot_tab,
    pre_tab,
    hot_rows,
    hidden,
    d_mixed,
    sums,
    grads,
    gain_sum,
    per_tile,
):
    tiles, _, tile = turned_hbm.shape
    slots, width = feat_tab.shape
    chips = slots // (cap * CORES)
    blocks = width // LANES
    per = cap * 2 * blocks
    groups = tile // LANES

    def span(t):
        return pl.ds(t * tile, tile)

    def load(t):
        return (
            pltpu.make_async_copy(pre_hbm.at[span(t)], pre.at[span(t)], per_tile.at[0, t]),
            pltpu.make_async_copy(cot_hbm.at[span(t)], cot.at[span(t)], per_tile.at[1, t]),
            pltpu.make_async_copy(turned_hbm.at[t], left.at[t, pl.ds(2 * slots, width)], per_tile.at[2, t]),
        )

    def leave(t):
        return pltpu.make_async_copy(d_preact.at[span(t)], d_preact_hbm.at[span(t)], per_tile.at[3, t])

    for t in range(tiles):
        for copy in load(t):
            copy.start()

    lane_ids = slot_ids(lax.broadcasted_iota(jnp.int32, (1, slots), 1), chips, cap)
    row_ids = slot_ids(lax.broadcasted_iota(jnp.int32, (slots, LANES), 0), chips, cap)

    def mark_rows(t):
        for g in range(groups):
            for at, ref in enumerate((send_ref, recv_ref)):
                upright = jnp.broadcast_to(ref[pl.ds(t * groups + g, 1), :], (LANES, LANES)).T
                for b in range(slots // LANES):
                    hot_rows[t % 2, g * LANES : (g + 1) * LANES, at * slots + b * LANES : at * slots + (b + 1) * LANES] = (
                        one_hot(upright, lane_ids[:, b * LANES : (b + 1) * LANES])
                    )

    def mark_cols(t):
        for g in range(groups):
            for at, ref in enumerate((send_ref, recv_ref)):
                left[t, at * slots : (at + 1) * slots, g * LANES : (g + 1) * LANES] = one_hot(
                    row_ids, ref[pl.ds(t * groups + g, 1), :]
                )

    sums[...] = jnp.zeros_like(sums)
    grads[3 * width : 4 * width, :] = jnp.zeros((width, width), F32)
    gain_sum[...] = jnp.zeros_like(gain_sum)
    rows32[...] = rows_ref[...].astype(F32)
    for core in range(CORES):
        for k in range(cap):
            at = (core * cap + k) * chips
            for j in range(blocks):
                cols = slice(j * LANES, (j + 1) * LANES)
                begin = core * per + k * 2 * blocks + j
                feat_tab[at : at + chips, cols] = rows32[pl.ds(begin, chips, stride=CORES * per), :].astype(BF)
                cot_tab[at : at + chips, cols] = rows32[
                    pl.ds(begin + blocks, chips, stride=CORES * per), :
                ].astype(BF)
    for part in range(2):
        pre_tab[part * slots : (part + 1) * slots, :] = dot(feat_tab[...], w_in[part + 1]).astype(BF)
    for copy in load(0):
        copy.wait()

    def gather(t):
        mark_rows(t)
        return pre[span(t), :].astype(F32) + dot(hot_rows[t % 2], pre_tab[...])

    def contract_output(t):
        grads[3 * width : 4 * width, :] += dot(hidden[t % 2], d_mixed[t % 2], ((0,), (0,)))

    def contract_input(t, c):
        lines = (2 * slots + width) // CHUNKS
        part = slice(c * lines, (c + 1) * lines)
        sums[part, :] += dot(left[t, part, :], d_preact[span(t), :])

    preact = gather(0)
    for t in range(tiles):
        if t:
            contract_output(t - 1)
        logistic = 0.5 * jnp.tanh(0.5 * preact) + 0.5
        silu = preact * logistic
        rounded = silu.astype(BF)
        hidden[t % 2] = rounded
        slope = logistic + silu * (1.0 - logistic)
        mixed = dot(rounded, w_out[...])
        found = dot(hot_rows[t % 2, :, slots:], cot_tab[...])
        if t:
            mark_cols(t - 1)
        for c in range(CHUNKS):
            if t:
                contract_input(t - 1, c)
            part = slice(c * (tile // CHUNKS), (c + 1) * (tile // CHUNKS))
            center = mixed[part] - jnp.mean(mixed[part], axis=1, keepdims=True)
            inverse = lax.rsqrt(jnp.mean(center * center, axis=1, keepdims=True) + 1e-5)
            normed = center * inverse
            scaled = (cot[pl.ds(t * tile + part.start, tile // CHUNKS), :].astype(F32) + found[part]) * gain_ref[...]
            product = scaled * normed
            d_mixed[t % 2, part, :] = (
                inverse
                * (
                    scaled
                    - jnp.mean(scaled, axis=1, keepdims=True)
                    - normed * jnp.mean(product, axis=1, keepdims=True)
                )
            ).astype(BF)
            gain_sum[...] += jnp.sum(product.reshape(-1, 8, width), axis=0)
        d_hidden = dot(d_mixed[t % 2], w_out[...], ((1,), (1,)))
        if t + 1 < tiles:
            for copy in load(t + 1):
                copy.wait()
            preact = gather(t + 1)
        d_preact[span(t), :] = (d_hidden * slope).astype(BF)
        leave(t).start()
    contract_output(tiles - 1)
    mark_cols(tiles - 1)
    for c in range(CHUNKS):
        contract_input(tiles - 1, c)

    sums_ref[...] = sums[0 : 2 * slots, :].astype(BF)
    grads[0:width, :] = sums[2 * slots :, :]
    for part in range(2):
        grads[(part + 1) * width : (part + 2) * width, :] = dot(
            feat_tab[...], sums_ref[part * slots : (part + 1) * slots, :], ((0,), (0,))
        )
    gain = jnp.sum(gain_sum[...], axis=0, keepdims=True) / gain_ref[...]
    core = core_ref[0]
    piece = 2 * width // chips
    body = piece * blocks
    for target, which in ((other_ref, 1 - core), (own_ref, core)):
        begin = pl.multiple_of(which * (2 * width), 2 * width)
        for j in range(blocks):
            target[:, j * piece : (j + 1) * piece, :] = (
                grads[pl.ds(begin, 2 * width), j * LANES : (j + 1) * LANES]
                .reshape(chips, piece, LANES)
                .astype(BF)
            )
        lines = [jnp.broadcast_to(gain[:, j * LANES : (j + 1) * LANES], (2, LANES)) for j in range(blocks)]
        target[:, body:, :] = jnp.broadcast_to(jnp.concatenate(lines, axis=0)[None].astype(BF), (chips, 8, LANES))
    for t in range(tiles):
        leave(t).wait()

def edge_pass(core, send_slot, recv_slot, gain, rows, w_input, w_output, pre, turned, cot, cap):
    edges, width = cot.shape
    tiles, _, tile = turned.shape
    devices = rows.shape[0] * LANES // (cap * 2 * width)
    slots = devices * cap
    chips = devices // CORES
    packets = jax.ShapeDtypeStruct((chips, 2 * width // chips * (width // LANES) + 8, LANES), BF)
    return pl.pallas_call(
        functools.partial(edge_kernel, cap),
        in_specs=[smem()] + [VMEM] * 6 + [HBM] * 3,
        out_specs=[HBM, VMEM, VMEM, VMEM],
        out_shape=[
            jax.ShapeDtypeStruct(cot.shape, BF),
            packets,
            packets,
            jax.ShapeDtypeStruct((2 * slots, width), BF),
        ],
        scratch_shapes=[
            pltpu.VMEM(rows.shape, F32),
            pltpu.VMEM(pre.shape, pre.dtype),
            pltpu.VMEM((tiles, 2 * slots + width, tile), BF),
            pltpu.VMEM(cot.shape, BF),
            pltpu.VMEM(cot.shape, BF),
            pltpu.VMEM((slots, width), BF),
            pltpu.VMEM((slots, width), BF),
            pltpu.VMEM((2 * slots, width), BF),
            pltpu.VMEM((2, tile, 2 * slots), BF),
            pltpu.VMEM((2, tile, width), BF),
            pltpu.VMEM((2, tile, width), BF),
            pltpu.VMEM((2 * slots + width, width), F32),
            pltpu.VMEM((4 * width, width), F32),
            pltpu.VMEM((8, width), F32),
            pltpu.SemaphoreType.DMA((4, tiles)),
        ],
        compiler_params=pltpu.CompilerParams(vmem_limit_bytes=BIG_VMEM),
        cost_estimate=cost(16 * edges * width * width, 8 * cot.size),
        name="edge_pass",
    )(core, send_slot, recv_slot, gain, rows, w_input, w_output, in_hbm(pre), in_hbm(turned), in_hbm(cot))

def back_kernel(cap, core_ref, sums_ref, w_ref, own_hbm, other_ref, tail, own, sem):
    slots = sums_ref.shape[0] // 2
    width = sums_ref.shape[1]
    chips = slots // (cap * CORES)
    blocks = width // LANES
    nodes = dot(sums_ref[0:slots, :], w_ref[1], ((1,), (1,))) + dot(
        sums_ref[slots : 2 * slots, :], w_ref[2], ((1,), (1,))
    )
    core = core_ref[0]
    tail[...] = jnp.zeros_like(tail)
    for side in range(CORES):
        for k in range(cap):
            at = (side * cap + k) * chips
            for j in range(blocks):
                tail[side, pl.ds(core * (cap * blocks) + k * blocks + j, chips, stride=CORES * cap * blocks), :] = (
                    nodes[at : at + chips, j * LANES : (j + 1) * LANES]
                )
    own[...] = tail[core].astype(BF).reshape(own.shape)
    copy = pltpu.make_async_copy(own, own_hbm, sem)
    copy.start()
    other_ref[...] = tail[1 - core].astype(BF).reshape(other_ref.shape)
    copy.wait()

def back_rows(core, sums, w_input, cap):
    slots, width = sums.shape[0] // 2, sums.shape[1]
    chips = slots // (cap * CORES)
    lines = CORES * cap * width // LANES
    return pl.pallas_call(
        functools.partial(back_kernel, cap),
        in_specs=[smem(), VMEM, VMEM],
        out_specs=[ANYWHERE, VMEM],
        out_shape=[jax.ShapeDtypeStruct((chips, lines, LANES), BF)] * 2,
        scratch_shapes=[
            pltpu.VMEM((CORES, chips * lines, LANES), F32),
            pltpu.VMEM((chips, lines, LANES), BF),
            pltpu.SemaphoreType.DMA,
        ],
        compiler_params=pltpu.CompilerParams(vmem_limit_bytes=BIG_VMEM),
        cost_estimate=cost(2 * sums.size * width, 6 * sums.size),
        name="back_rows",
    )(core, sums, w_input)

def merge_kernel(own_ref, got_ref, out_ref):
    out_ref[...] = own_ref[...] + got_ref[...]


def merge(own, got):
    return pl.pallas_call(
        merge_kernel,
        in_specs=[VMEM, VMEM],
        out_specs=VMEM,
        out_shape=jax.ShapeDtypeStruct(own.shape, BF),
        compiler_params=pltpu.CompilerParams(vmem_limit_bytes=BIG_VMEM),
        cost_estimate=cost(own.size, 6 * own.size),
        name="merge",
    )(own, got)


def reduce_kernel(factor, in_ref, own_hbm, got_ref, out_ref, gain_ref, own, sem):
    copy = pltpu.make_async_copy(own_hbm, own, sem)
    copy.start()
    total = jnp.sum(in_ref[...].astype(F32), axis=0) * factor
    body = total.shape[0] - 8
    out_ref[:, 0:body, :] = jnp.broadcast_to(total[0:body].astype(BF)[None], (in_ref.shape[0], body, LANES))
    gain_ref[...] = jnp.concatenate([total[body + 2 * j : body + 2 * j + 1] for j in range(4)], axis=1)
    copy.wait()
    out_ref[:, body:, :] = own[...] + got_ref[...]

def reduce_packets(packets, own, got, factor):
    chips, lines, _ = packets.shape
    return pl.pallas_call(
        functools.partial(reduce_kernel, factor),
        out_shape=[
            jax.ShapeDtypeStruct((chips, lines - 8 + own.shape[1], LANES), BF),
            jax.ShapeDtypeStruct((1, 4 * LANES), F32),
        ],
        in_specs=[VMEM, ANYWHERE, VMEM],
        out_specs=[VMEM, VMEM],
        scratch_shapes=[pltpu.VMEM(own.shape, BF), pltpu.SemaphoreType.DMA],
        compiler_params=pltpu.CompilerParams(vmem_limit_bytes=BIG_VMEM),
        cost_estimate=cost(packets.size, 4 * packets.size),
        name="reduce_packets",
    )(packets, in_hbm(own), got)

def node_kernel(asked_ref, packets_ref, cots_ref, out_ref, ends, rows, hots):
    devices, cap = asked_ref.shape
    nodes, width = cots_ref.shape
    blocks = width // LANES
    body = packets_ref.shape[1] - CORES * cap * blocks
    ends[...] = packets_ref[:, body:, :].astype(F32).reshape(ends.shape)
    spot = lax.broadcasted_iota(jnp.int32, (devices, nodes), 1)
    for k in range(cap):
        at = k * devices
        hots[at : at + devices, :] = one_hot(asked_ref[:, k : k + 1], spot)
        for j in range(blocks):
            rows[at : at + devices, j * LANES : (j + 1) * LANES] = ends[
                pl.ds(k * blocks + j, devices, stride=cap * blocks), :
            ].astype(BF)
    sums = dot(hots[...], rows[...], ((0,), (0,)))
    out_ref[...] = (cots_ref[...].astype(F32) + sums).astype(BF)

def node_grads(asked, packets, cots):
    devices, cap = asked.shape
    nodes, width = cots.shape
    slots = devices * cap
    return pl.pallas_call(
        node_kernel,
        out_shape=jax.ShapeDtypeStruct(cots.shape, BF),
        scratch_shapes=[
            pltpu.VMEM((slots * width // LANES, LANES), F32),
            pltpu.VMEM((slots, width), BF),
            pltpu.VMEM((slots, nodes), BF),
        ],
        compiler_params=pltpu.CompilerParams(vmem_limit_bytes=BIG_VMEM),
        cost_estimate=cost(2 * slots * cots.size, 4 * cots.size + 2 * packets.size),
        name="node_grads",
    )(asked, packets, cots)

def unpack_kernel(is_mine, core_ref, packets_ref, *refs):
    input_ref, output_ref, values, sems = refs[-4:]
    width = output_ref.shape[1]
    blocks = width // LANES
    chips = packets_ref.shape[0]
    piece = 2 * width // chips
    half = core_ref[0] if is_mine else 1 - core_ref[0]

    def copy(upper, a):
        if not upper:
            target = input_ref.at[pl.ds(a * width, width)]
        else:
            target = output_ref if a else input_ref.at[pl.ds(2 * width, width)]
        return pltpu.make_async_copy(values.at[pl.ds(a * width, width)], target, sems.at[a])

    for a in range(2):
        chunk = slice(a * (chips // 2), (a + 1) * (chips // 2))
        for j in range(blocks):
            values[a * width : (a + 1) * width, j * LANES : (j + 1) * LANES] = (
                packets_ref[chunk, j * piece : (j + 1) * piece, :].astype(F32).reshape(width, LANES)
            )

        @pl.when(half == 0)
        def _():
            copy(False, a).start()

        @pl.when(half != 0)
        def _():
            copy(True, a).start()

    for a in range(2):

        @pl.when(half == 0)
        def _():
            copy(False, a).wait()

        @pl.when(half != 0)
        def _():
            copy(True, a).wait()

def unpack(is_mine, core, packets, width, earlier=()):
    return pl.pallas_call(
        functools.partial(unpack_kernel, is_mine),
        in_specs=[smem(), VMEM] + [ANYWHERE] * len(earlier),
        out_specs=[ANYWHERE] * 2,
        out_shape=[
            jax.ShapeDtypeStruct((3 * width, width), F32),
            jax.ShapeDtypeStruct((width, width), F32),
        ],
        scratch_shapes=[pltpu.VMEM((2 * width, width), F32), pltpu.SemaphoreType.DMA((2,))],
        input_output_aliases={2 + a: a for a in range(len(earlier))},
        compiler_params=pltpu.CompilerParams(vmem_limit_bytes=BIG_VMEM),
        cost_estimate=cost(packets.size, 6 * packets.size),
        name="unpack_mine" if is_mine else "unpack_other",
    )(core, packets, *earlier)

def on_device(
    edge_feats,
    node_feats,
    edge_cot,
    node_cot,
    requests,
    send_slot,
    recv_slot,
    w_input,
    w_output,
    norm_gain,
):
    chips, cores = lax.axis_size("chip"), lax.axis_size("core")
    devices = chips * cores
    both = ("chip", "core")
    cap = requests.shape[1] // devices
    edges, width = edge_feats.shape
    core = lax.axis_index("core").astype(jnp.int32).reshape(1)
    pairs = [(d, d ^ 1) for d in range(devices)]

    asked = lax.all_to_all(
        requests.reshape(devices, 1, cap), both, split_axis=0, concat_axis=0, tiled=True
    ).reshape(devices, cap)
    picked = pick_rows(asked, node_feats, node_cot).reshape(devices, -1, LANES)
    rows = lax.all_to_all(picked, both, split_axis=0, concat_axis=0, tiled=True).reshape(-1, LANES)
    pre, turned = prep_pass(edge_feats, w_input, TILE)
    d_preact, own, other, sums = edge_pass(
        core,
        send_slot,
        recv_slot,
        norm_gain.reshape(1, width),
        rows,
        w_input,
        w_output,
        pre,
        turned,
        edge_cot,
        cap,
    )
    got = lax.ppermute(other, both, pairs)
    back_own, back_other = back_rows(core, sums, w_input, cap)
    got, back_own, back_other = lax.optimization_barrier((got, back_own, back_other))
    packets = lax.all_to_all(merge(own, got), "chip", split_axis=0, concat_axis=0, tiled=True)
    back_got = lax.ppermute(back_other, both, pairs)
    factor = float(edges * devices) ** (-0.5)
    pieces, gain = reduce_packets(packets, back_own, back_got, factor)
    d_preact, pieces = lax.optimization_barrier((d_preact, pieces))
    mine = lax.all_to_all(pieces, "chip", split_axis=0, concat_axis=0, tiled=True)
    grad_edges = grad_pass(d_preact, w_input, edge_cot, 1024)
    grad_edges, mine = lax.optimization_barrier((grad_edges, mine))
    partner = lax.ppermute(mine, both, pairs)
    grad_nodes = node_grads(asked, mine, node_cot)
    grads = unpack(True, core, mine, width)
    grad_input, grad_output = unpack(False, core, partner, width, grads)
    return (
        grad_edges,
        grad_nodes,
        grad_input.reshape(3, width, width),
        grad_output,
        gain.reshape(width),
    )

def solution(mesh):
    pairs = Mesh(mesh.devices.reshape(-1, CORES), ("chip", "core"))
    rows = P(("chip", "core"), None)
    return jax.shard_map(
        on_device,
        mesh=pairs,
        in_specs=(rows,) * 7 + (P(),) * 3,
        out_specs=(rows, rows, P(), P(), P()),
        check_vma=False,
    )
```

```python
import functools

import jax
import jax.numpy as jnp
from jax import lax
from jax.experimental import pallas as pl
from jax.experimental.pallas import tpu as pltpu
from jax.sharding import Mesh, PartitionSpec as P

BF = jnp.bfloat16
F32 = jnp.float32
LANES = 128
CORES = 2
TILE = 768
CHUNKS = 2
PRE = F32
BIG_VMEM = 48 * 1024 * 1024

VMEM = pl.BlockSpec(memory_space=pltpu.VMEM)
ANYWHERE = pl.BlockSpec(memory_space=pl.ANY)
HBM = pl.BlockSpec(memory_space=pltpu.HBM)

def dot(left, right, over=((1,), (0,))):
    return lax.dot_general(left, right, (over, ((), ())), preferred_element_type=F32)

def in_hbm(array):
    return pltpu.with_memory_space_constraint(array, pltpu.HBM)

def smem():
    return pl.BlockSpec(memory_space=pltpu.SMEM)

def cost(flops, moved):
    return pl.CostEstimate(flops=flops, bytes_accessed=moved, transcendentals=0)

def one_hot(left, right):
    return jnp.where(left == right, 1.0, 0.0).astype(BF)

def pick_kernel(asked_ref, feats_hbm, cots_hbm, out_ref, feats, cots, rows, sems):
    devices, cap = asked_ref.shape
    nodes, width = feats.shape
    blocks = width // LANES
    per = cap * 2 * blocks
    copies = [
        pltpu.make_async_copy(feats_hbm, feats, sems.at[0]),
        pltpu.make_async_copy(cots_hbm, cots, sems.at[1]),
    ]
    for copy in copies:
        copy.start()
    spot = lax.broadcasted_iota(jnp.int32, (devices, nodes), 1)
    hots = [one_hot(asked_ref[:, k : k + 1], spot) for k in range(cap)]
    for at, table in enumerate((feats, cots)):
        copies[at].wait()
        for k in range(cap):
            found = dot(hots[k], table[...])
            for j in range(blocks):
                rows[pl.ds(k * 2 * blocks + at * blocks + j, devices, stride=per), :] = found[
                    :, j * LANES : (j + 1) * LANES
                ]
    out_ref[...] = rows[...].astype(BF)

def pick_rows(asked, feats, cots):
    devices, cap = asked.shape
    width = feats.shape[1]
    total = devices * cap * 2 * width // LANES
    return pl.pallas_call(
        pick_kernel,
        in_specs=[VMEM, HBM, HBM],
        out_specs=VMEM,
        out_shape=jax.ShapeDtypeStruct((total, LANES), BF),
        scratch_shapes=[
            pltpu.VMEM(feats.shape, BF),
            pltpu.VMEM(cots.shape, BF),
            pltpu.VMEM((total, LANES), F32),
            pltpu.SemaphoreType.DMA((2,)),
        ],
        compiler_params=pltpu.CompilerParams(vmem_limit_bytes=BIG_VMEM),
        cost_estimate=cost(4 * devices * cap * feats.size, 4 * total * LANES),
        name="pick_rows",
    )(asked, in_hbm(feats), in_hbm(cots))

def slot_ids(position, chips, cap):
    half = cap * chips
    core = jnp.where(position >= half, 1, 0)
    rest = position - core * half
    k = jnp.where(rest >= chips, 1, 0) + jnp.where(rest >= 2 * chips, 1, 0)
    chip = rest - k * chips
    return chip * (CORES * cap) + core * cap + k

def prep_kernel(feats_ref, w_ref, pre_ref, turned_ref):
    feats = feats_ref[...]
    pre_ref[...] = dot(feats, w_ref[0]).astype(PRE)
    turned_ref[0] = feats.T

def prep_pass(feats, w_input, tile):
    edges, width = feats.shape
    tiles = edges // tile
    rows = pl.BlockSpec((tile, width), lambda i: (i, 0))
    return pl.pallas_call(
        prep_kernel,
        grid=(tiles,),
        in_specs=[rows, pl.BlockSpec((1, width, width), lambda i: (0, 0, 0))],
        out_specs=[rows, pl.BlockSpec((1, width, tile), lambda i: (i, 0, 0))],
        out_shape=[
            jax.ShapeDtypeStruct((edges, width), PRE),
            jax.ShapeDtypeStruct((tiles, width, tile), BF),
        ],
        compiler_params=pltpu.CompilerParams(vmem_limit_bytes=BIG_VMEM),
        cost_estimate=cost(2 * edges * width * width, 8 * feats.size),
        name="prep_pass",
    )(feats, w_input)

def grad_kernel(d_preact_ref, w_ref, cot_ref, out_ref):
    grad = dot(d_preact_ref[...], w_ref[0], ((1,), (1,)))
    out_ref[...] = (cot_ref[...].astype(F32) + grad).astype(BF)

def grad_pass(d_preact, w_input, cot, tile):
    edges, width = cot.shape
    tiles = pl.BlockSpec((tile, width), lambda i: (i, 0))
    return pl.pallas_call(
        grad_kernel,
        grid=(edges // tile,),
        in_specs=[tiles, pl.BlockSpec((1, width, width), lambda i: (0, 0, 0)), tiles],
        out_specs=tiles,
        out_shape=jax.ShapeDtypeStruct(cot.shape, BF),
        cost_estimate=cost(2 * edges * width * width, 6 * cot.size),
        name="grad_pass",
    )(in_hbm(d_preact), w_input, in_hbm(cot))

def edge_kernel(
    cap,
    core_ref,
    send_ref,
    recv_ref,
    gain_ref,
    rows_ref,
    w_in,
    w_out,
    pre_hbm,
    turned_hbm,
    cot_hbm,
    d_preact_hbm,
    own_ref,
    other_ref,
    sums_ref,
    rows32,
    pre,
    left,
    cot,
    d_preact,
    feat_tab,
    cot_tab,
    pre_tab,
    hot_rows,
    hidden,
    d_mixed,
    sums,
    grads,
    gain_sum,
    per_tile,
):
    tiles, _, tile = turned_hbm.shape
    slots, width = feat_tab.shape
    chips = slots // (cap * CORES)
    blocks = width // LANES
    per = cap * 2 * blocks
    groups = tile // LANES

    def span(t):
        return pl.ds(t * tile, tile)

    def load(t):
        return (
            pltpu.make_async_copy(pre_hbm.at[span(t)], pre.at[span(t)], per_tile.at[0, t]),
            pltpu.make_async_copy(cot_hbm.at[span(t)], cot.at[span(t)], per_tile.at[1, t]),
            pltpu.make_async_copy(turned_hbm.at[t], left.at[t, pl.ds(2 * slots, width)], per_tile.at[2, t]),
        )

    def leave(t):
        return pltpu.make_async_copy(d_preact.at[span(t)], d_preact_hbm.at[span(t)], per_tile.at[3, t])

    for t in range(tiles):
        for copy in load(t):
            copy.start()

    lane_ids = slot_ids(lax.broadcasted_iota(jnp.int32, (1, slots), 1), chips, cap)
    row_ids = slot_ids(lax.broadcasted_iota(jnp.int32, (slots, LANES), 0), chips, cap)

    def mark_rows(t):
        for g in range(groups):
            for at, ref in enumerate((send_ref, recv_ref)):
                upright = jnp.broadcast_to(ref[pl.ds(t * groups + g, 1), :], (LANES, LANES)).T
                for b in range(slots // LANES):
                    hot_rows[t % 2, g * LANES : (g + 1) * LANES, at * slots + b * LANES : at * slots + (b + 1) * LANES] = (
                        one_hot(upright, lane_ids[:, b * LANES : (b + 1) * LANES])
                    )

    def mark_cols(t):
        for g in range(groups):
            for at, ref in enumerate((send_ref, recv_ref)):
                left[t, at * slots : (at + 1) * slots, g * LANES : (g + 1) * LANES] = one_hot(
                    row_ids, ref[pl.ds(t * groups + g, 1), :]
                )

    sums[...] = jnp.zeros_like(sums)
    grads[3 * width : 4 * width, :] = jnp.zeros((width, width), F32)
    gain_sum[...] = jnp.zeros_like(gain_sum)
    rows32[...] = rows_ref[...].astype(F32)
    for core in range(CORES):
        for k in range(cap):
            at = (core * cap + k) * chips
            for j in range(blocks):
                cols = slice(j * LANES, (j + 1) * LANES)
                begin = core * per + k * 2 * blocks + j
                feat_tab[at : at + chips, cols] = rows32[pl.ds(begin, chips, stride=CORES * per), :].astype(BF)
                cot_tab[at : at + chips, cols] = rows32[
                    pl.ds(begin + blocks, chips, stride=CORES * per), :
                ].astype(BF)
    for part in range(2):
        pre_tab[part * slots : (part + 1) * slots, :] = dot(feat_tab[...], w_in[part + 1]).astype(BF)
    for copy in load(0):
        copy.wait()

    def gather(t):
        mark_rows(t)
        return pre[span(t), :].astype(F32) + dot(hot_rows[t % 2], pre_tab[...])

    def contract_output(t):
        grads[3 * width : 4 * width, :] += dot(hidden[t % 2], d_mixed[t % 2], ((0,), (0,)))

    def contract_input(t, c):
        lines = (2 * slots + width) // CHUNKS
        part = slice(c * lines, (c + 1) * lines)
        sums[part, :] += dot(left[t, part, :], d_preact[span(t), :])

    preact = gather(0)
    for t in range(tiles):
        if t:
            contract_output(t - 1)
        logistic = 0.5 * jnp.tanh(0.5 * preact) + 0.5
        silu = preact * logistic
        rounded = silu.astype(BF)
        hidden[t % 2] = rounded
        slope = logistic + silu * (1.0 - logistic)
        mixed = dot(rounded, w_out[...])
        found = dot(hot_rows[t % 2, :, slots:], cot_tab[...])
        if t:
            mark_cols(t - 1)
        for c in range(CHUNKS):
            if t:
                contract_input(t - 1, c)
            part = slice(c * (tile // CHUNKS), (c + 1) * (tile // CHUNKS))
            center = mixed[part] - jnp.mean(mixed[part], axis=1, keepdims=True)
            inverse = lax.rsqrt(jnp.mean(center * center, axis=1, keepdims=True) + 1e-5)
            normed = center * inverse
            scaled = (cot[pl.ds(t * tile + part.start, tile // CHUNKS), :].astype(F32) + found[part]) * gain_ref[...]
            product = scaled * normed
            d_mixed[t % 2, part, :] = (
                inverse
                * (
                    scaled
                    - jnp.mean(scaled, axis=1, keepdims=True)
                    - normed * jnp.mean(product, axis=1, keepdims=True)
                )
            ).astype(BF)
            gain_sum[...] += jnp.sum(product.reshape(-1, 8, width), axis=0)
        d_hidden = dot(d_mixed[t % 2], w_out[...], ((1,), (1,)))
        if t + 1 < tiles:
            for copy in load(t + 1):
                copy.wait()
            preact = gather(t + 1)
        d_preact[span(t), :] = (d_hidden * slope).astype(BF)
        leave(t).start()
    contract_output(tiles - 1)
    mark_cols(tiles - 1)
    for c in range(CHUNKS):
        contract_input(tiles - 1, c)

    sums_ref[...] = sums[0 : 2 * slots, :].astype(BF)
    grads[0:width, :] = sums[2 * slots :, :]
    for part in range(2):
        grads[(part + 1) * width : (part + 2) * width, :] = dot(
            feat_tab[...], sums_ref[part * slots : (part + 1) * slots, :], ((0,), (0,))
        )
    gain = jnp.sum(gain_sum[...], axis=0, keepdims=True) / gain_ref[...]
    core = core_ref[0]
    piece = 2 * width // chips
    body = piece * blocks
    for target, which in ((other_ref, 1 - core), (own_ref, core)):
        begin = pl.multiple_of(which * (2 * width), 2 * width)
        for j in range(blocks):
            target[:, j * piece : (j + 1) * piece, :] = (
                grads[pl.ds(begin, 2 * width), j * LANES : (j + 1) * LANES]
                .reshape(chips, piece, LANES)
                .astype(BF)
            )
        lines = [jnp.broadcast_to(gain[:, j * LANES : (j + 1) * LANES], (2, LANES)) for j in range(blocks)]
        target[:, body:, :] = jnp.broadcast_to(jnp.concatenate(lines, axis=0)[None].astype(BF), (chips, 8, LANES))
    for t in range(tiles):
        leave(t).wait()

def edge_pass(core, send_slot, recv_slot, gain, rows, w_input, w_output, pre, turned, cot, cap):
    edges, width = cot.shape
    tiles, _, tile = turned.shape
    devices = rows.shape[0] * LANES // (cap * 2 * width)
    slots = devices * cap
    chips = devices // CORES
    packets = jax.ShapeDtypeStruct((chips, 2 * width // chips * (width // LANES) + 8, LANES), BF)
    return pl.pallas_call(
        functools.partial(edge_kernel, cap),
        in_specs=[smem()] + [VMEM] * 6 + [HBM] * 3,
        out_specs=[HBM, VMEM, VMEM, VMEM],
        out_shape=[
            jax.ShapeDtypeStruct(cot.shape, BF),
            packets,
            packets,
            jax.ShapeDtypeStruct((2 * slots, width), BF),
        ],
        scratch_shapes=[
            pltpu.VMEM(rows.shape, F32),
            pltpu.VMEM(pre.shape, pre.dtype),
            pltpu.VMEM((tiles, 2 * slots + width, tile), BF),
            pltpu.VMEM(cot.shape, BF),
            pltpu.VMEM(cot.shape, BF),
            pltpu.VMEM((slots, width), BF),
            pltpu.VMEM((slots, width), BF),
            pltpu.VMEM((2 * slots, width), BF),
            pltpu.VMEM((2, tile, 2 * slots), BF),
            pltpu.VMEM((2, tile, width), BF),
            pltpu.VMEM((2, tile, width), BF),
            pltpu.VMEM((2 * slots + width, width), F32),
            pltpu.VMEM((4 * width, width), F32),
            pltpu.VMEM((8, width), F32),
            pltpu.SemaphoreType.DMA((4, tiles)),
        ],
        compiler_params=pltpu.CompilerParams(vmem_limit_bytes=BIG_VMEM),
        cost_estimate=cost(16 * edges * width * width, 8 * cot.size),
        name="edge_pass",
    )(core, send_slot, recv_slot, gain, rows, w_input, w_output, in_hbm(pre), in_hbm(turned), in_hbm(cot))

def back_kernel(cap, core_ref, sums_ref, w_ref, own_hbm, other_ref, tail, own, sem):
    slots = sums_ref.shape[0] // 2
    width = sums_ref.shape[1]
    chips = slots // (cap * CORES)
    blocks = width // LANES
    nodes = dot(sums_ref[0:slots, :], w_ref[1], ((1,), (1,))) + dot(
        sums_ref[slots : 2 * slots, :], w_ref[2], ((1,), (1,))
    )
    core = core_ref[0]
    tail[...] = jnp.zeros_like(tail)
    for side in range(CORES):
        for k in range(cap):
            at = (side * cap + k) * chips
            for j in range(blocks):
                tail[side, pl.ds(core * (cap * blocks) + k * blocks + j, chips, stride=CORES * cap * blocks), :] = (
                    nodes[at : at + chips, j * LANES : (j + 1) * LANES]
                )
    own[...] = tail[core].astype(BF).reshape(own.shape)
    copy = pltpu.make_async_copy(own, own_hbm, sem)
    copy.start()
    other_ref[...] = tail[1 - core].astype(BF).reshape(other_ref.shape)
    copy.wait()

def back_rows(core, sums, w_input, cap):
    slots, width = sums.shape[0] // 2, sums.shape[1]
    chips = slots // (cap * CORES)
    lines = CORES * cap * width // LANES
    return pl.pallas_call(
        functools.partial(back_kernel, cap),
        in_specs=[smem(), VMEM, VMEM],
        out_specs=[ANYWHERE, VMEM],
        out_shape=[jax.ShapeDtypeStruct((chips, lines, LANES), BF)] * 2,
        scratch_shapes=[
            pltpu.VMEM((CORES, chips * lines, LANES), F32),
            pltpu.VMEM((chips, lines, LANES), BF),
            pltpu.SemaphoreType.DMA,
        ],
        compiler_params=pltpu.CompilerParams(vmem_limit_bytes=BIG_VMEM),
        cost_estimate=cost(2 * sums.size * width, 6 * sums.size),
        name="back_rows",
    )(core, sums, w_input)

def merge_kernel(own_ref, got_ref, out_ref):
    out_ref[...] = own_ref[...] + got_ref[...]


def merge(own, got):
    return pl.pallas_call(
        merge_kernel,
        in_specs=[VMEM, VMEM],
        out_specs=VMEM,
        out_shape=jax.ShapeDtypeStruct(own.shape, BF),
        compiler_params=pltpu.CompilerParams(vmem_limit_bytes=BIG_VMEM),
        cost_estimate=cost(own.size, 6 * own.size),
        name="merge",
    )(own, got)


def tail_kernel(own_ref, got_ref, out_ref):
    out_ref[:, out_ref.shape[1] - own_ref.shape[1] :, :] = own_ref[...] + got_ref[...]


def tail_packets(own, got, body):
    chips, lines, _ = own.shape
    return pl.pallas_call(
        tail_kernel,
        out_shape=jax.ShapeDtypeStruct((chips, body + lines, LANES), BF),
        compiler_params=pltpu.CompilerParams(vmem_limit_bytes=BIG_VMEM),
        cost_estimate=cost(own.size, 10 * own.size),
        name="tail_packets",
    )(own, got)


def reduce_kernel(factor, in_ref, tails_hbm, out_hbm, gain_ref, piece, sems):
    del tails_hbm
    body = piece.shape[0]
    total = jnp.sum(in_ref[...].astype(F32), axis=0) * factor
    piece[...] = total[0:body].astype(BF)
    copies = [
        pltpu.make_async_copy(piece, out_hbm.at[chip, pl.ds(0, body)], sems.at[chip])
        for chip in range(in_ref.shape[0])
    ]
    for copy in copies:
        copy.start()
    gain_ref[...] = jnp.concatenate([total[body + 2 * j : body + 2 * j + 1] for j in range(4)], axis=1)
    for copy in copies:
        copy.wait()


def reduce_packets(packets, tails, factor):
    chips, lines, _ = packets.shape
    return pl.pallas_call(
        functools.partial(reduce_kernel, factor),
        out_shape=[
            jax.ShapeDtypeStruct(tails.shape, BF),
            jax.ShapeDtypeStruct((1, 4 * LANES), F32),
        ],
        in_specs=[VMEM, HBM],
        out_specs=[HBM, VMEM],
        scratch_shapes=[pltpu.VMEM((lines - 8, LANES), BF), pltpu.SemaphoreType.DMA((chips,))],
        input_output_aliases={1: 0},
        compiler_params=pltpu.CompilerParams(vmem_limit_bytes=BIG_VMEM),
        cost_estimate=cost(packets.size, 4 * packets.size),
        name="reduce_packets",
    )(packets, in_hbm(tails))


def node_sums(asked_ref, packets_ref, cots_ref, out_ref, ends, rows, hots):
    devices, cap = asked_ref.shape
    nodes, width = cots_ref.shape
    blocks = width // LANES
    body = packets_ref.shape[1] - CORES * cap * blocks
    ends[...] = packets_ref[:, body:, :].astype(F32).reshape(ends.shape)
    spot = lax.broadcasted_iota(jnp.int32, (devices, nodes), 1)
    for k in range(cap):
        at = k * devices
        hots[at : at + devices, :] = one_hot(asked_ref[:, k : k + 1], spot)
        for j in range(blocks):
            rows[at : at + devices, j * LANES : (j + 1) * LANES] = ends[
                pl.ds(k * blocks + j, devices, stride=cap * blocks), :
            ].astype(BF)
    sums = dot(hots[...], rows[...], ((0,), (0,)))
    out_ref[...] = (cots_ref[...].astype(F32) + sums).astype(BF)


def spread(half, packets_ref, input_ref, output_ref, values, sems):
    width = output_ref.shape[1]
    blocks = width // LANES
    chips = packets_ref.shape[0]
    piece = 2 * width // chips

    def copy(upper, a):
        if not upper:
            target = input_ref.at[pl.ds(a * width, width)]
        else:
            target = output_ref if a else input_ref.at[pl.ds(2 * width, width)]
        return pltpu.make_async_copy(values.at[pl.ds(a * width, width)], target, sems.at[a])

    for a in range(2):
        chunk = slice(a * (chips // 2), (a + 1) * (chips // 2))
        for j in range(blocks):
            values[a * width : (a + 1) * width, j * LANES : (j + 1) * LANES] = (
                packets_ref[chunk, j * piece : (j + 1) * piece, :].astype(F32).reshape(width, LANES)
            )

        @pl.when(half == 0)
        def _():
            copy(False, a).start()

        @pl.when(half != 0)
        def _():
            copy(True, a).start()

    def finish():
        for a in range(2):

            @pl.when(half == 0)
            def _():
                copy(False, a).wait()

            @pl.when(half != 0)
            def _():
                copy(True, a).wait()

    return finish


def mine_kernel(core_ref, packets_ref, asked_ref, cots_ref, input_ref, output_ref, nodes_ref, values, sems, *work):
    finish = spread(core_ref[0], packets_ref, input_ref, output_ref, values, sems)
    node_sums(asked_ref, packets_ref, cots_ref, nodes_ref, *work)
    finish()


def other_kernel(core_ref, packets_ref, _, __, input_ref, output_ref, values, sems):
    spread(1 - core_ref[0], packets_ref, input_ref, output_ref, values, sems)()


def unpack_mine(core, packets, asked, cots):
    devices, cap = asked.shape
    nodes, width = cots.shape
    slots = devices * cap
    return pl.pallas_call(
        mine_kernel,
        in_specs=[smem(), VMEM, VMEM, VMEM],
        out_specs=[HBM, HBM, VMEM],
        out_shape=[
            jax.ShapeDtypeStruct((3 * width, width), F32),
            jax.ShapeDtypeStruct((width, width), F32),
            jax.ShapeDtypeStruct(cots.shape, BF),
        ],
        scratch_shapes=[
            pltpu.VMEM((2 * width, width), F32),
            pltpu.SemaphoreType.DMA((2,)),
            pltpu.VMEM((slots * width // LANES, LANES), F32),
            pltpu.VMEM((slots, width), BF),
            pltpu.VMEM((slots, nodes), BF),
        ],
        compiler_params=pltpu.CompilerParams(vmem_limit_bytes=BIG_VMEM),
        cost_estimate=cost(2 * slots * cots.size, 6 * packets.size),
        name="unpack_mine",
    )(core, packets, asked, cots)


def unpack_other(core, packets, grad_input, grad_output):
    return pl.pallas_call(
        other_kernel,
        in_specs=[smem(), VMEM, HBM, HBM],
        out_specs=[HBM, HBM],
        out_shape=[
            jax.ShapeDtypeStruct(grad_input.shape, F32),
            jax.ShapeDtypeStruct(grad_output.shape, F32),
        ],
        scratch_shapes=[
            pltpu.VMEM((2 * grad_output.shape[0], grad_output.shape[1]), F32),
            pltpu.SemaphoreType.DMA((2,)),
        ],
        input_output_aliases={2: 0, 3: 1},
        compiler_params=pltpu.CompilerParams(vmem_limit_bytes=BIG_VMEM),
        cost_estimate=cost(packets.size, 6 * packets.size),
        name="unpack_other",
    )(core, packets, grad_input, grad_output)


def on_device(
    edge_feats,
    node_feats,
    edge_cot,
    node_cot,
    requests,
    send_slot,
    recv_slot,
    w_input,
    w_output,
    norm_gain,
):
    chips, cores = lax.axis_size("chip"), lax.axis_size("core")
    devices = chips * cores
    both = ("chip", "core")
    cap = requests.shape[1] // devices
    edges, width = edge_feats.shape
    core = lax.axis_index("core").astype(jnp.int32).reshape(1)
    pairs = [(d, d ^ 1) for d in range(devices)]

    asked = lax.all_to_all(
        requests.reshape(devices, 1, cap), both, split_axis=0, concat_axis=0, tiled=True
    ).reshape(devices, cap)
    picked = pick_rows(asked, node_feats, node_cot).reshape(devices, -1, LANES)
    rows = lax.all_to_all(picked, both, split_axis=0, concat_axis=0, tiled=True).reshape(-1, LANES)
    pre, turned = prep_pass(edge_feats, w_input, TILE)
    d_preact, own, other, sums = edge_pass(
        core,
        send_slot,
        recv_slot,
        norm_gain.reshape(1, width),
        rows,
        w_input,
        w_output,
        pre,
        turned,
        edge_cot,
        cap,
    )
    got = lax.ppermute(other, both, pairs)
    back_own, back_other = back_rows(core, sums, w_input, cap)
    got, back_own, back_other = lax.optimization_barrier((got, back_own, back_other))
    packets = lax.all_to_all(merge(own, got), "chip", split_axis=0, concat_axis=0, tiled=True)
    back_got = lax.ppermute(back_other, both, pairs)
    factor = float(edges * devices) ** (-0.5)
    tails = tail_packets(back_own, back_got, packets.shape[1] - 8)
    pieces, gain = reduce_packets(packets, tails, factor)
    d_preact, pieces = lax.optimization_barrier((d_preact, pieces))
    mine = lax.all_to_all(pieces, "chip", split_axis=0, concat_axis=0, tiled=True)
    grad_edges = grad_pass(d_preact, w_input, edge_cot, 1024)
    grad_edges, mine = lax.optimization_barrier((grad_edges, mine))
    partner = lax.ppermute(mine, both, pairs)
    grad_input, grad_output, grad_nodes = unpack_mine(core, mine, asked, node_cot)
    grad_input, grad_output = unpack_other(core, partner, grad_input, grad_output)
    return (
        grad_edges,
        grad_nodes,
        grad_input.reshape(3, width, width),
        grad_output,
        gain.reshape(width),
    )

def solution(mesh):
    pairs = Mesh(mesh.devices.reshape(-1, CORES), ("chip", "core"))
    rows = P(("chip", "core"), None)
    return jax.shard_map(
        on_device,
        mesh=pairs,
        in_specs=(rows,) * 7 + (P(),) * 3,
        out_specs=(rows, rows, P(), P(), P()),
        check_vma=False,
    )
```

```python
import functools

import jax
import jax.numpy as jnp
from jax import lax
from jax.experimental import pallas as pl
from jax.experimental.pallas import tpu as pltpu
from jax.sharding import Mesh, PartitionSpec as P

BF = jnp.bfloat16
F32 = jnp.float32
LANES = 128
CORES = 2
TILE = 768
CHUNKS = 2
PRE = F32
BIG_VMEM = 48 * 1024 * 1024

VMEM = pl.BlockSpec(memory_space=pltpu.VMEM)
ANYWHERE = pl.BlockSpec(memory_space=pl.ANY)
HBM = pl.BlockSpec(memory_space=pltpu.HBM)

def dot(left, right, over=((1,), (0,))):
    return lax.dot_general(left, right, (over, ((), ())), preferred_element_type=F32)

def in_hbm(array):
    return pltpu.with_memory_space_constraint(array, pltpu.HBM)

def smem():
    return pl.BlockSpec(memory_space=pltpu.SMEM)

def cost(flops, moved):
    return pl.CostEstimate(flops=flops, bytes_accessed=moved, transcendentals=0)

def one_hot(left, right):
    return jnp.where(left == right, 1.0, 0.0).astype(BF)

def stage_kernel(feats_hbm, cots_hbm, feats_ref, cots_ref, sems):
    copies = [
        pltpu.make_async_copy(feats_hbm, feats_ref, sems.at[0]),
        pltpu.make_async_copy(cots_hbm, cots_ref, sems.at[1]),
    ]
    for copy in copies:
        copy.start()
    for copy in copies:
        copy.wait()


def stage(feats, cots):
    return pl.pallas_call(
        stage_kernel,
        in_specs=[HBM, HBM],
        out_specs=[VMEM, VMEM],
        out_shape=[jax.ShapeDtypeStruct(feats.shape, BF), jax.ShapeDtypeStruct(cots.shape, BF)],
        scratch_shapes=[pltpu.SemaphoreType.DMA((2,))],
        compiler_params=pltpu.CompilerParams(vmem_limit_bytes=BIG_VMEM),
        cost_estimate=cost(0, 8 * feats.size),
        name="stage",
    )(in_hbm(feats), in_hbm(cots))


def pick_kernel(asked_ref, feats_ref, cots_ref, out_ref, rows):
    devices, cap = asked_ref.shape
    nodes, width = feats_ref.shape
    blocks = width // LANES
    per = cap * 2 * blocks
    spot = lax.broadcasted_iota(jnp.int32, (devices, nodes), 1)
    for k in range(cap):
        hot = one_hot(asked_ref[:, k : k + 1], spot)
        for at, table in enumerate((feats_ref, cots_ref)):
            found = dot(hot, table[...])
            for j in range(blocks):
                rows[pl.ds(k * 2 * blocks + at * blocks + j, devices, stride=per), :] = found[
                    :, j * LANES : (j + 1) * LANES
                ]
    out_ref[...] = rows[...].astype(BF)


def pick_rows(asked, feats, cots):
    devices, cap = asked.shape
    width = feats.shape[1]
    total = devices * cap * 2 * width // LANES
    return pl.pallas_call(
        pick_kernel,
        in_specs=[VMEM] * 3,
        out_specs=VMEM,
        out_shape=jax.ShapeDtypeStruct((total, LANES), BF),
        scratch_shapes=[pltpu.VMEM((total, LANES), F32)],
        compiler_params=pltpu.CompilerParams(vmem_limit_bytes=BIG_VMEM),
        cost_estimate=cost(4 * devices * cap * feats.size, 4 * total * LANES),
        name="pick_rows",
    )(asked, feats, cots)


def slot_ids(position, chips, cap):
    half = cap * chips
    core = jnp.where(position >= half, 1, 0)
    rest = position - core * half
    k = jnp.where(rest >= chips, 1, 0) + jnp.where(rest >= 2 * chips, 1, 0)
    chip = rest - k * chips
    return chip * (CORES * cap) + core * cap + k

def prep_kernel(feats_ref, w_ref, pre_ref, turned_ref):
    feats = feats_ref[...]
    pre_ref[...] = dot(feats, w_ref[0]).astype(PRE)
    turned_ref[0] = feats.T

def prep_pass(feats, w_input, tile):
    edges, width = feats.shape
    tiles = edges // tile
    rows = pl.BlockSpec((tile, width), lambda i: (i, 0))
    return pl.pallas_call(
        prep_kernel,
        grid=(tiles,),
        in_specs=[rows, pl.BlockSpec((1, width, width), lambda i: (0, 0, 0))],
        out_specs=[rows, pl.BlockSpec((1, width, tile), lambda i: (i, 0, 0))],
        out_shape=[
            jax.ShapeDtypeStruct((edges, width), PRE),
            jax.ShapeDtypeStruct((tiles, width, tile), BF),
        ],
        compiler_params=pltpu.CompilerParams(vmem_limit_bytes=BIG_VMEM),
        cost_estimate=cost(2 * edges * width * width, 8 * feats.size),
        name="prep_pass",
    )(feats, w_input)

def grad_kernel(d_preact_ref, w_ref, cot_ref, out_ref):
    grad = dot(d_preact_ref[...], w_ref[0], ((1,), (1,)))
    out_ref[...] = (cot_ref[...].astype(F32) + grad).astype(BF)

def grad_pass(d_preact, w_input, cot, tile):
    edges, width = cot.shape
    tiles = pl.BlockSpec((tile, width), lambda i: (i, 0))
    return pl.pallas_call(
        grad_kernel,
        grid=(edges // tile,),
        in_specs=[tiles, pl.BlockSpec((1, width, width), lambda i: (0, 0, 0)), tiles],
        out_specs=tiles,
        out_shape=jax.ShapeDtypeStruct(cot.shape, BF),
        cost_estimate=cost(2 * edges * width * width, 6 * cot.size),
        name="grad_pass",
    )(in_hbm(d_preact), w_input, in_hbm(cot))

def edge_kernel(
    cap,
    core_ref,
    send_ref,
    recv_ref,
    gain_ref,
    rows_ref,
    w_in,
    w_out,
    pre_hbm,
    turned_hbm,
    cot_hbm,
    d_preact_hbm,
    own_ref,
    other_ref,
    sums_ref,
    rows32,
    pre,
    left,
    cot,
    d_preact,
    feat_tab,
    cot_tab,
    pre_tab,
    hot_rows,
    hidden,
    d_mixed,
    sums,
    grads,
    gain_sum,
    per_tile,
):
    tiles, _, tile = turned_hbm.shape
    slots, width = feat_tab.shape
    chips = slots // (cap * CORES)
    blocks = width // LANES
    per = cap * 2 * blocks
    groups = tile // LANES

    def span(t):
        return pl.ds(t * tile, tile)

    def load(t):
        return (
            pltpu.make_async_copy(pre_hbm.at[span(t)], pre.at[span(t)], per_tile.at[0, t]),
            pltpu.make_async_copy(cot_hbm.at[span(t)], cot.at[span(t)], per_tile.at[1, t]),
            pltpu.make_async_copy(turned_hbm.at[t], left.at[t, pl.ds(2 * slots, width)], per_tile.at[2, t]),
        )

    def leave(t):
        return pltpu.make_async_copy(d_preact.at[span(t)], d_preact_hbm.at[span(t)], per_tile.at[3, t])

    for t in range(tiles):
        for copy in load(t):
            copy.start()

    lane_ids = slot_ids(lax.broadcasted_iota(jnp.int32, (1, slots), 1), chips, cap)
    row_ids = slot_ids(lax.broadcasted_iota(jnp.int32, (slots, LANES), 0), chips, cap)

    def mark_rows(t):
        for g in range(groups):
            for at, ref in enumerate((send_ref, recv_ref)):
                upright = jnp.broadcast_to(ref[pl.ds(t * groups + g, 1), :], (LANES, LANES)).T
                for b in range(slots // LANES):
                    hot_rows[t % 2, g * LANES : (g + 1) * LANES, at * slots + b * LANES : at * slots + (b + 1) * LANES] = (
                        one_hot(upright, lane_ids[:, b * LANES : (b + 1) * LANES])
                    )

    def mark_cols(t):
        for g in range(groups):
            for at, ref in enumerate((send_ref, recv_ref)):
                left[t, at * slots : (at + 1) * slots, g * LANES : (g + 1) * LANES] = one_hot(
                    row_ids, ref[pl.ds(t * groups + g, 1), :]
                )

    sums[...] = jnp.zeros_like(sums)
    grads[3 * width : 4 * width, :] = jnp.zeros((width, width), F32)
    gain_sum[...] = jnp.zeros_like(gain_sum)
    rows32[...] = rows_ref[...].astype(F32)
    for core in range(CORES):
        for k in range(cap):
            at = (core * cap + k) * chips
            for j in range(blocks):
                cols = slice(j * LANES, (j + 1) * LANES)
                begin = core * per + k * 2 * blocks + j
                feat_tab[at : at + chips, cols] = rows32[pl.ds(begin, chips, stride=CORES * per), :].astype(BF)
                cot_tab[at : at + chips, cols] = rows32[
                    pl.ds(begin + blocks, chips, stride=CORES * per), :
                ].astype(BF)
    for part in range(2):
        pre_tab[part * slots : (part + 1) * slots, :] = dot(feat_tab[...], w_in[part + 1]).astype(BF)
    for copy in load(0):
        copy.wait()

    def gather(t):
        mark_rows(t)
        return pre[span(t), :].astype(F32) + dot(hot_rows[t % 2], pre_tab[...])

    def contract_output(t):
        grads[3 * width : 4 * width, :] += dot(hidden[t % 2], d_mixed[t % 2], ((0,), (0,)))

    def contract_input(t, c):
        lines = (2 * slots + width) // CHUNKS
        part = slice(c * lines, (c + 1) * lines)
        sums[part, :] += dot(left[t, part, :], d_preact[span(t), :])

    preact = gather(0)
    for t in range(tiles):
        if t:
            contract_output(t - 1)
        logistic = 0.5 * jnp.tanh(0.5 * preact) + 0.5
        silu = preact * logistic
        rounded = silu.astype(BF)
        hidden[t % 2] = rounded
        slope = logistic + silu * (1.0 - logistic)
        mixed = dot(rounded, w_out[...])
        found = dot(hot_rows[t % 2, :, slots:], cot_tab[...])
        if t:
            mark_cols(t - 1)
        for c in range(CHUNKS):
            if t:
                contract_input(t - 1, c)
            part = slice(c * (tile // CHUNKS), (c + 1) * (tile // CHUNKS))
            center = mixed[part] - jnp.mean(mixed[part], axis=1, keepdims=True)
            inverse = lax.rsqrt(jnp.mean(center * center, axis=1, keepdims=True) + 1e-5)
            normed = center * inverse
            scaled = (cot[pl.ds(t * tile + part.start, tile // CHUNKS), :].astype(F32) + found[part]) * gain_ref[...]
            product = scaled * normed
            d_mixed[t % 2, part, :] = (
                inverse
                * (
                    scaled
                    - jnp.mean(scaled, axis=1, keepdims=True)
                    - normed * jnp.mean(product, axis=1, keepdims=True)
                )
            ).astype(BF)
            gain_sum[...] += jnp.sum(product.reshape(-1, 8, width), axis=0)
        d_hidden = dot(d_mixed[t % 2], w_out[...], ((1,), (1,)))
        if t + 1 < tiles:
            for copy in load(t + 1):
                copy.wait()
            preact = gather(t + 1)
        d_preact[span(t), :] = (d_hidden * slope).astype(BF)
        leave(t).start()
    contract_output(tiles - 1)
    mark_cols(tiles - 1)
    for c in range(CHUNKS):
        contract_input(tiles - 1, c)

    sums_ref[...] = sums[0 : 2 * slots, :].astype(BF)
    grads[0:width, :] = sums[2 * slots :, :]
    for part in range(2):
        grads[(part + 1) * width : (part + 2) * width, :] = dot(
            feat_tab[...], sums_ref[part * slots : (part + 1) * slots, :], ((0,), (0,))
        )
    gain = jnp.sum(gain_sum[...], axis=0, keepdims=True) / gain_ref[...]
    core = core_ref[0]
    piece = 2 * width // chips
    body = piece * blocks
    for target, which in ((other_ref, 1 - core), (own_ref, core)):
        begin = pl.multiple_of(which * (2 * width), 2 * width)
        for j in range(blocks):
            target[:, j * piece : (j + 1) * piece, :] = (
                grads[pl.ds(begin, 2 * width), j * LANES : (j + 1) * LANES]
                .reshape(chips, piece, LANES)
                .astype(BF)
            )
        lines = [jnp.broadcast_to(gain[:, j * LANES : (j + 1) * LANES], (2, LANES)) for j in range(blocks)]
        target[:, body:, :] = jnp.broadcast_to(jnp.concatenate(lines, axis=0)[None].astype(BF), (chips, 8, LANES))
    for t in range(tiles):
        leave(t).wait()

def edge_pass(core, send_slot, recv_slot, gain, rows, w_input, w_output, pre, turned, cot, cap):
    edges, width = cot.shape
    tiles, _, tile = turned.shape
    devices = rows.shape[0] * LANES // (cap * 2 * width)
    slots = devices * cap
    chips = devices // CORES
    packets = jax.ShapeDtypeStruct((chips, 2 * width // chips * (width // LANES) + 8, LANES), BF)
    return pl.pallas_call(
        functools.partial(edge_kernel, cap),
        in_specs=[smem()] + [VMEM] * 6 + [HBM] * 3,
        out_specs=[HBM, VMEM, VMEM, VMEM],
        out_shape=[
            jax.ShapeDtypeStruct(cot.shape, BF),
            packets,
            packets,
            jax.ShapeDtypeStruct((2 * slots, width), BF),
        ],
        scratch_shapes=[
            pltpu.VMEM(rows.shape, F32),
            pltpu.VMEM(pre.shape, pre.dtype),
            pltpu.VMEM((tiles, 2 * slots + width, tile), BF),
            pltpu.VMEM(cot.shape, BF),
            pltpu.VMEM(cot.shape, BF),
            pltpu.VMEM((slots, width), BF),
            pltpu.VMEM((slots, width), BF),
            pltpu.VMEM((2 * slots, width), BF),
            pltpu.VMEM((2, tile, 2 * slots), BF),
            pltpu.VMEM((2, tile, width), BF),
            pltpu.VMEM((2, tile, width), BF),
            pltpu.VMEM((2 * slots + width, width), F32),
            pltpu.VMEM((4 * width, width), F32),
            pltpu.VMEM((8, width), F32),
            pltpu.SemaphoreType.DMA((4, tiles)),
        ],
        compiler_params=pltpu.CompilerParams(vmem_limit_bytes=BIG_VMEM),
        cost_estimate=cost(16 * edges * width * width, 8 * cot.size),
        name="edge_pass",
    )(core, send_slot, recv_slot, gain, rows, w_input, w_output, in_hbm(pre), in_hbm(turned), in_hbm(cot))

def back_kernel(cap, core_ref, sums_ref, w_ref, own_hbm, other_ref, tail, own, sem):
    slots = sums_ref.shape[0] // 2
    width = sums_ref.shape[1]
    chips = slots // (cap * CORES)
    blocks = width // LANES
    nodes = dot(sums_ref[0:slots, :], w_ref[1], ((1,), (1,))) + dot(
        sums_ref[slots : 2 * slots, :], w_ref[2], ((1,), (1,))
    )
    core = core_ref[0]
    tail[...] = jnp.zeros_like(tail)
    for side in range(CORES):
        for k in range(cap):
            at = (side * cap + k) * chips
            for j in range(blocks):
                tail[side, pl.ds(core * (cap * blocks) + k * blocks + j, chips, stride=CORES * cap * blocks), :] = (
                    nodes[at : at + chips, j * LANES : (j + 1) * LANES]
                )
    own[...] = tail[core].astype(BF).reshape(own.shape)
    copy = pltpu.make_async_copy(own, own_hbm, sem)
    copy.start()
    other_ref[...] = tail[1 - core].astype(BF).reshape(other_ref.shape)
    copy.wait()

def back_rows(core, sums, w_input, cap):
    slots, width = sums.shape[0] // 2, sums.shape[1]
    chips = slots // (cap * CORES)
    lines = CORES * cap * width // LANES
    return pl.pallas_call(
        functools.partial(back_kernel, cap),
        in_specs=[smem(), VMEM, VMEM],
        out_specs=[ANYWHERE, VMEM],
        out_shape=[jax.ShapeDtypeStruct((chips, lines, LANES), BF)] * 2,
        scratch_shapes=[
            pltpu.VMEM((CORES, chips * lines, LANES), F32),
            pltpu.VMEM((chips, lines, LANES), BF),
            pltpu.SemaphoreType.DMA,
        ],
        compiler_params=pltpu.CompilerParams(vmem_limit_bytes=BIG_VMEM),
        cost_estimate=cost(2 * sums.size * width, 6 * sums.size),
        name="back_rows",
    )(core, sums, w_input)

def merge_kernel(own_ref, got_ref, out_ref):
    out_ref[...] = own_ref[...] + got_ref[...]


def merge(own, got):
    return pl.pallas_call(
        merge_kernel,
        in_specs=[VMEM, VMEM],
        out_specs=VMEM,
        out_shape=jax.ShapeDtypeStruct(own.shape, BF),
        compiler_params=pltpu.CompilerParams(vmem_limit_bytes=BIG_VMEM),
        cost_estimate=cost(own.size, 6 * own.size),
        name="merge",
    )(own, got)


def tail_kernel(own_ref, got_ref, out_ref):
    out_ref[:, out_ref.shape[1] - own_ref.shape[1] :, :] = own_ref[...] + got_ref[...]


def tail_packets(own, got, body):
    chips, lines, _ = own.shape
    return pl.pallas_call(
        tail_kernel,
        out_shape=jax.ShapeDtypeStruct((chips, body + lines, LANES), BF),
        compiler_params=pltpu.CompilerParams(vmem_limit_bytes=BIG_VMEM),
        cost_estimate=cost(own.size, 10 * own.size),
        name="tail_packets",
    )(own, got)


def reduce_kernel(factor, in_ref, tails_hbm, out_hbm, gain_ref, piece, sems):
    del tails_hbm
    body = piece.shape[0]
    total = jnp.sum(in_ref[...].astype(F32), axis=0) * factor
    piece[...] = total[0:body].astype(BF)
    copies = [
        pltpu.make_async_copy(piece, out_hbm.at[chip, pl.ds(0, body)], sems.at[chip])
        for chip in range(in_ref.shape[0])
    ]
    for copy in copies:
        copy.start()
    gain_ref[...] = jnp.concatenate([total[body + 2 * j : body + 2 * j + 1] for j in range(4)], axis=1)
    for copy in copies:
        copy.wait()


def reduce_packets(packets, tails, factor):
    chips, lines, _ = packets.shape
    return pl.pallas_call(
        functools.partial(reduce_kernel, factor),
        out_shape=[
            jax.ShapeDtypeStruct(tails.shape, BF),
            jax.ShapeDtypeStruct((1, 4 * LANES), F32),
        ],
        in_specs=[VMEM, HBM],
        out_specs=[HBM, VMEM],
        scratch_shapes=[pltpu.VMEM((lines - 8, LANES), BF), pltpu.SemaphoreType.DMA((chips,))],
        input_output_aliases={1: 0},
        compiler_params=pltpu.CompilerParams(vmem_limit_bytes=BIG_VMEM),
        cost_estimate=cost(packets.size, 4 * packets.size),
        name="reduce_packets",
    )(packets, in_hbm(tails))


def node_sums(asked_ref, packets_ref, cots_ref, out_ref, ends, rows, hots):
    devices, cap = asked_ref.shape
    nodes, width = cots_ref.shape
    blocks = width // LANES
    body = packets_ref.shape[1] - CORES * cap * blocks
    ends[...] = packets_ref[:, body:, :].astype(F32).reshape(ends.shape)
    spot = lax.broadcasted_iota(jnp.int32, (devices, nodes), 1)
    for k in range(cap):
        at = k * devices
        hots[at : at + devices, :] = one_hot(asked_ref[:, k : k + 1], spot)
        for j in range(blocks):
            rows[at : at + devices, j * LANES : (j + 1) * LANES] = ends[
                pl.ds(k * blocks + j, devices, stride=cap * blocks), :
            ].astype(BF)
    sums = dot(hots[...], rows[...], ((0,), (0,)))
    out_ref[...] = (cots_ref[...].astype(F32) + sums).astype(BF)


def spread(half, packets_ref, input_ref, output_ref, values, sems):
    width = output_ref.shape[1]
    blocks = width // LANES
    chips = packets_ref.shape[0]
    piece = 2 * width // chips

    def copy(upper, a):
        if not upper:
            target = input_ref.at[pl.ds(a * width, width)]
        else:
            target = output_ref if a else input_ref.at[pl.ds(2 * width, width)]
        return pltpu.make_async_copy(values.at[pl.ds(a * width, width)], target, sems.at[a])

    for a in range(2):
        chunk = slice(a * (chips // 2), (a + 1) * (chips // 2))
        for j in range(blocks):
            values[a * width : (a + 1) * width, j * LANES : (j + 1) * LANES] = (
                packets_ref[chunk, j * piece : (j + 1) * piece, :].astype(F32).reshape(width, LANES)
            )

        @pl.when(half == 0)
        def _():
            copy(False, a).start()

        @pl.when(half != 0)
        def _():
            copy(True, a).start()

    def finish():
        for a in range(2):

            @pl.when(half == 0)
            def _():
                copy(False, a).wait()

            @pl.when(half != 0)
            def _():
                copy(True, a).wait()

    return finish


def mine_kernel(core_ref, packets_ref, asked_ref, cots_ref, input_ref, output_ref, nodes_ref, values, sems, *work):
    finish = spread(core_ref[0], packets_ref, input_ref, output_ref, values, sems)
    node_sums(asked_ref, packets_ref, cots_ref, nodes_ref, *work)
    finish()


def other_kernel(core_ref, packets_ref, _, __, input_ref, output_ref, values, sems):
    spread(1 - core_ref[0], packets_ref, input_ref, output_ref, values, sems)()


def unpack_mine(core, packets, asked, cots):
    devices, cap = asked.shape
    nodes, width = cots.shape
    slots = devices * cap
    return pl.pallas_call(
        mine_kernel,
        in_specs=[smem(), VMEM, VMEM, VMEM],
        out_specs=[HBM, HBM, VMEM],
        out_shape=[
            jax.ShapeDtypeStruct((3 * width, width), F32),
            jax.ShapeDtypeStruct((width, width), F32),
            jax.ShapeDtypeStruct(cots.shape, BF),
        ],
        scratch_shapes=[
            pltpu.VMEM((2 * width, width), F32),
            pltpu.SemaphoreType.DMA((2,)),
            pltpu.VMEM((slots * width // LANES, LANES), F32),
            pltpu.VMEM((slots, width), BF),
            pltpu.VMEM((slots, nodes), BF),
        ],
        compiler_params=pltpu.CompilerParams(vmem_limit_bytes=BIG_VMEM),
        cost_estimate=cost(2 * slots * cots.size, 6 * packets.size),
        name="unpack_mine",
    )(core, packets, asked, cots)


def unpack_other(core, packets, grad_input, grad_output):
    return pl.pallas_call(
        other_kernel,
        in_specs=[smem(), VMEM, HBM, HBM],
        out_specs=[HBM, HBM],
        out_shape=[
            jax.ShapeDtypeStruct(grad_input.shape, F32),
            jax.ShapeDtypeStruct(grad_output.shape, F32),
        ],
        scratch_shapes=[
            pltpu.VMEM((2 * grad_output.shape[0], grad_output.shape[1]), F32),
            pltpu.SemaphoreType.DMA((2,)),
        ],
        input_output_aliases={2: 0, 3: 1},
        compiler_params=pltpu.CompilerParams(vmem_limit_bytes=BIG_VMEM),
        cost_estimate=cost(packets.size, 6 * packets.size),
        name="unpack_other",
    )(core, packets, grad_input, grad_output)


def on_device(
    edge_feats,
    node_feats,
    edge_cot,
    node_cot,
    requests,
    send_slot,
    recv_slot,
    w_input,
    w_output,
    norm_gain,
):
    chips, cores = lax.axis_size("chip"), lax.axis_size("core")
    devices = chips * cores
    both = ("chip", "core")
    cap = requests.shape[1] // devices
    edges, width = edge_feats.shape
    core = lax.axis_index("core").astype(jnp.int32).reshape(1)
    pairs = [(d, d ^ 1) for d in range(devices)]

    asked = lax.all_to_all(
        requests.reshape(devices, 1, cap), both, split_axis=0, concat_axis=0, tiled=True
    ).reshape(devices, cap)
    picked = pick_rows(asked, *stage(node_feats, node_cot)).reshape(devices, -1, LANES)
    rows = lax.all_to_all(picked, both, split_axis=0, concat_axis=0, tiled=True).reshape(-1, LANES)
    pre, turned = prep_pass(edge_feats, w_input, TILE)
    d_preact, own, other, sums = edge_pass(
        core,
        send_slot,
        recv_slot,
        norm_gain.reshape(1, width),
        rows,
        w_input,
        w_output,
        pre,
        turned,
        edge_cot,
        cap,
    )
    got = lax.ppermute(other, both, pairs)
    back_own, back_other = back_rows(core, sums, w_input, cap)
    got, back_own, back_other = lax.optimization_barrier((got, back_own, back_other))
    packets = lax.all_to_all(merge(own, got), "chip", split_axis=0, concat_axis=0, tiled=True)
    back_got = lax.ppermute(back_other, both, pairs)
    factor = float(edges * devices) ** (-0.5)
    tails = tail_packets(back_own, back_got, packets.shape[1] - 8)
    pieces, gain = reduce_packets(packets, tails, factor)
    d_preact, pieces = lax.optimization_barrier((d_preact, pieces))
    mine = lax.all_to_all(pieces, "chip", split_axis=0, concat_axis=0, tiled=True)
    grad_edges = grad_pass(d_preact, w_input, edge_cot, 1024)
    grad_edges, mine = lax.optimization_barrier((grad_edges, mine))
    partner = lax.ppermute(mine, both, pairs)
    grad_input, grad_output, grad_nodes = unpack_mine(core, mine, asked, node_cot)
    grad_input, grad_output = unpack_other(core, partner, grad_input, grad_output)
    return (
        grad_edges,
        grad_nodes,
        grad_input.reshape(3, width, width),
        grad_output,
        gain.reshape(width),
    )

def solution(mesh):
    pairs = Mesh(mesh.devices.reshape(-1, CORES), ("chip", "core"))
    rows = P(("chip", "core"), None)
    return jax.shard_map(
        on_device,
        mesh=pairs,
        in_specs=(rows,) * 7 + (P(),) * 3,
        out_specs=(rows, rows, P(), P(), P()),
        check_vma=False,
    )
```
